256 devices in a mesh: dp: 32 (over z, x), expert: 8 (over y, core).
Axes of the slice: x: 4, y: 4, z: 8, core: 2. Of those that a mesh axis runs over, the one named last changes fastest.
Arguments:
- tokens: bfloat16 [4096, 4096], P('dp'), may hold values from -6 to 6
- expert_ids: int32 [4096, 8], P('dp'), may hold values from 0 to 63, all different within a row; in each aligned block of 128 rows (0 to 127, 128 to 255, ...) at most 20 rows name the same one
- gates: float32 [4096, 8], P('dp'), may hold values from 0.02 to 0.25
- w_gate: bfloat16 [64, 1536, 4096], P('dp', 'expert'), may hold values from -0.09375 to 0.09375
- w_up: bfloat16 [64, 1536, 4096], P('dp', 'expert'), may hold values from -0.09375 to 0.09375
- w_down: bfloat16 [64, 1536, 4096], P('dp', 'expert'), may hold values from -0.15625 to 0.15625
- gate_scale: float32 [64, 1536], P('dp', 'expert'), may hold values from 0.5 to 2
- up_scale: float32 [64, 1536], P('dp', 'expert'), may hold values from 0.5 to 2
- down_scale: float32 [64, 4096], P('dp'), may hold values from 0.5 to 2
- kv_rows: bfloat16 [4096, 1024], P('dp', 'expert'), may hold values from -6 to 6
- page_slots: int32 [128], replicated, may hold values from 0 to 127, each once
Outputs:
- moe_out: bfloat16 [4096, 4096], P('dp', 'expert')
- kv_cache: bfloat16 [128, 32, 1024], P('dp', None, 'expert')
The draws below stay inside these ranges and needn't reach their ends.
Inputs may be any that keep to these rules, and one draw needn't show every extreme that they name: `expert_ids`: in the 128 rows of one index of dp, no expert is named by more than 20 rows. `page_slots`: each cache page is named once; cache page c lies on index c // 4 of dp.
All inputs are finite; a program needn't handle non-finite values.
Results may differ from the reference program's by a relative error of at most 0.02.
Values may be sent and summed in bfloat16 or wider, within the bound.
No kernel may reach another device: no remote copies, remote signals or barrier semaphores. Data moves between devices by JAX's collectives and lax.ppermute only.
A program may use at most 128 MiB of HBM per device.

```python
import math
import jax
import jax.numpy as jnp
import numpy as np
from jax import lax

D = 4096
H = 1536
KV_WIDTH = 1024
TOP = 8
PAGE = 32
TOK_DEV = 128
TOKENS = 4096
EXPERTS = 64
CAP = 20
HID_DEV = 192
PAGES = 128
N_DP = 32
N_EXPERT = 8


def level_of(stream_key, extent, cuts, low, top_value):
    gain = 1.0
    for dim, blocks in cuts:
        steps = jax.random.uniform(jax.random.fold_in(jax.random.fold_in(stream_key, 6), dim), (blocks,), jnp.float32, low / len(cuts), top_value / len(cuts))
        gain = gain * jnp.repeat(jnp.exp(steps), extent[dim] // blocks).reshape((-1,) + (1,) * (len(extent) - 1 - dim))
    return gain


def routed_block(key, own, number, rows, number_of, top, most, skew):
    order = jax.random.permutation(key, number_of)
    packed, common = portions_of(number_of, rows * top, most, skew, True), portions_of(number_of, rows * top, most, skew, False)
    places = jnp.arange(number_of)

    def named(sizes, rotation):
        used = int((sizes > 0).sum())
        fixed = max(1, used // 4)
        moved = fixed + (places - fixed + rotation * (used - fixed)) % max(1, number_of - fixed)
        return jnp.zeros((number_of,), jnp.int32).at[order[jnp.where(places < fixed, places, moved)]].set(jnp.asarray(sizes, jnp.int32))

    sizes = jnp.where(number % 4 == 0, named(packed, number // 4), named(common, number - number // 4 - 1))
    mixed = jax.random.permutation(jax.random.fold_in(own, 3), number_of)
    source_of, receiver = mixed[0:number_of // 2 * 2:2], mixed[1:number_of // 2 * 2:2]
    margin = jnp.minimum(sizes[source_of] - 1, most - sizes[receiver]) // 2
    margin = jnp.where((source_of == order[0]) | (receiver == order[0]) | (sizes[receiver] == 0), 0, jnp.maximum(margin, 0))
    moved = jax.random.randint(jax.random.fold_in(own, 4), (number_of // 2,), 0, 1 << 20) % (margin + 1)
    sizes = sizes.at[source_of].add(-moved).at[receiver].add(moved)
    labels = jnp.searchsorted(jnp.cumsum(sizes), jnp.arange(rows * top), side="right").astype(jnp.int32)
    listing = labels.reshape(top, rows).T
    listing = listing[jax.random.permutation(jax.random.fold_in(own, 1), rows)]
    rotation = jax.random.randint(jax.random.fold_in(own, 2), (rows, 1), 0, top)
    return jnp.take_along_axis(listing, (jnp.arange(top)[None, :] + rotation) % top, axis=1)


def portions_of(number_of, total, reach, lean, full):
    weights = [(1 << 20) // math.isqrt(standing ** lean) + 1 for standing in range(1, number_of + 1)]
    largest = reach if full else min(reach, max(-(-total // number_of), total * weights[0] // sum(weights)))
    least = 1 if total - largest >= number_of - 1 else 0
    given, spare = [largest] + [least] * (number_of - 1), total - largest - least * (number_of - 1)
    while spare > 0:
        movable = [i for i in range(1, number_of) if given[i] < largest] or [i for i in range(1, number_of) if given[i] < reach]
        mass, budget = sum([weights[i] for i in movable]), spare
        for i in movable:
            more = min(reach - given[i], max(1, budget * weights[i] // mass), spare)
            given[i] = given[i] + more
            spare = spare - more
    return np.array(given)


def gaussian(rng, dims, width, reach, shards=(), kind=jnp.bfloat16):
    drawn = width * jax.random.normal(rng, dims, jnp.float32)
    if shards:
        drawn = drawn * level_of(rng, dims, shards, -0.22, 0.18)
    return jnp.clip(drawn, -reach, reach).astype(kind)


def setup_inputs(seed: int = 0) -> dict:
    keys = jax.random.split(jax.random.key(seed), 12)
    tokens = gaussian(keys[0], (TOKENS, D), 1.0, 6.0, ((0, 32),))
    expert_ids_keys = jax.random.split(jax.random.fold_in(keys[1], 1), TOKENS // TOK_DEV)
    expert_ids_turns = jax.random.permutation(jax.random.fold_in(keys[1], 3), TOKENS // TOK_DEV)
    expert_ids = jax.vmap(lambda own, number: routed_block(jax.random.fold_in(keys[1], 2), own, number, TOK_DEV, EXPERTS, TOP, CAP, 2))(expert_ids_keys, expert_ids_turns).reshape((TOKENS, TOP))
    gates = jnp.clip(0.02 + 0.23 * jax.random.uniform(keys[2], (TOKENS, TOP), jnp.float32) ** level_of(keys[2], (TOKENS, TOP), ((0, 32),), -0.2, 0.2), 0.02, 0.25)
    w_gate = gaussian(keys[3], (EXPERTS, H, D), D ** -0.5, 0.09375, ((0, 32), (1, 8)))
    w_up = gaussian(keys[4], (EXPERTS, H, D), D ** -0.5, 0.09375, ((0, 32), (1, 8)))
    w_down = gaussian(keys[5], (EXPERTS, H, D), H ** -0.5, 0.15625, ((0, 32), (1, 8)))
    gate_scale = jnp.clip(jnp.exp(math.log(2.0) - 1.3862944 * jax.random.uniform(keys[6], (EXPERTS, H), jnp.float32) ** level_of(keys[6], (EXPERTS, H), ((0, 32), (1, 8)), -0.2, 0.2)), 0.5, 2.0)
    up_scale = jnp.clip(jnp.exp(math.log(2.0) - 1.3862944 * jax.random.uniform(keys[7], (EXPERTS, H), jnp.float32) ** level_of(keys[7], (EXPERTS, H), ((0, 32), (1, 8)), -0.2, 0.2)), 0.5, 2.0)
    down_scale = jnp.clip(jnp.exp(math.log(2.0) - 1.3862944 * jax.random.uniform(keys[8], (EXPERTS, D), jnp.float32) ** level_of(keys[8], (EXPERTS, D), ((0, 32),), -0.2, 0.2)), 0.5, 2.0)
    kv_rows = gaussian(keys[9], (TOKENS, KV_WIDTH), 1.0, 6.0, ((0, 32), (1, 8)))
    page_slots = jax.random.permutation(keys[10], PAGES).astype(jnp.int32)
    return {"tokens": tokens, "expert_ids": expert_ids, "gates": gates, "w_gate": w_gate, "w_up": w_up, "w_down": w_down, "gate_scale": gate_scale, "up_scale": up_scale, "down_scale": down_scale, "kv_rows": kv_rows, "page_slots": page_slots}


def slot_index(expert_ids):
    flat = expert_ids.reshape(N_DP, TOK_DEV * TOP)
    onehot = (flat[:, :, None] == jnp.arange(EXPERTS, dtype=jnp.int32)[None, None, :]).astype(jnp.int32)
    ranks = jnp.cumsum(onehot, axis=1) - 1
    position = jnp.sum(ranks * onehot, axis=2).astype(jnp.int32)
    source = jnp.arange(N_DP, dtype=jnp.int32)[:, None]
    return ((flat * N_DP + source) * CAP + position).reshape(TOKENS, TOP).astype(jnp.int32)


def expert_block(args):
    rows, wg, wu, wd, sg, su, sd = args
    gate_act = jnp.dot(rows, wg.T, preferred_element_type=jnp.float32) * sg[None, :]
    up_act = jnp.dot(rows, wu.T, preferred_element_type=jnp.float32) * su[None, :]
    hidden = (jax.nn.silu(gate_act) * up_act).astype(jnp.bfloat16)
    grouped = hidden.reshape(rows.shape[0], N_EXPERT, HID_DEV).astype(jnp.float32)
    down_groups = wd.reshape(N_EXPERT, HID_DEV, D).astype(jnp.float32)
    parts = jnp.einsum("rgh,ghd->grd", grouped, down_groups) * sd[None, None, :]
    parts = parts.astype(jnp.bfloat16).astype(jnp.float32)
    return jnp.sum(parts, axis=0)


def reference(tokens, expert_ids, gates, w_gate, w_up, w_down, gate_scale, up_scale, down_scale, kv_rows, page_slots):
    dest = slot_index(expert_ids)
    token_of = (jnp.arange(TOKENS * TOP, dtype=jnp.int32) // TOP).astype(jnp.int32)
    slot_token = jnp.full((EXPERTS * N_DP * CAP,), TOKENS, dtype=jnp.int32).at[dest.reshape(-1)].set(token_of)
    padded = jnp.concatenate([tokens, jnp.zeros((1, D), tokens.dtype)], axis=0)
    buffer = padded[slot_token].reshape(EXPERTS, N_DP * CAP, D)
    expert_out = lax.map(expert_block, (buffer, w_gate, w_up, w_down, gate_scale, up_scale, down_scale))
    expert_out = expert_out.reshape(EXPERTS * N_DP * CAP, D)
    total = jnp.zeros((TOKENS, D), jnp.float32)
    for pick in range(TOP):
        total = total + gates[:, pick][:, None] * expert_out[dest[:, pick]]
    moe_out = total.astype(jnp.bfloat16)
    pages = kv_rows.reshape(PAGES, PAGE, KV_WIDTH)
    kv_cache = jnp.zeros((PAGES, PAGE, KV_WIDTH), kv_rows.dtype).at[page_slots].set(pages)
    return moe_out, kv_cache
```

```python
import functools

import jax
import jax.numpy as jnp
import numpy as np
from jax import lax
from jax.experimental import pallas as pl
from jax.experimental.pallas import tpu as pltpu
from jax.sharding import Mesh
from jax.sharding import PartitionSpec as P

BF = jnp.bfloat16
F32 = jnp.float32
PAGE = 32
ROWS = 8
DP = ("z", "x")
MOVES = ((0, False), (0, True), (1, False), (1, True), (3, False), (3, True), (2, False), (2, True))


def dot(a, b):
    return lax.dot_general(a, b, (((1,), (0,)), ((), ())), preferred_element_type=F32)


def dot_nt(a, b):
    return lax.dot_general(a, b, (((1,), (1,)), ((), ())), preferred_element_type=F32)


def dot_tn(a, b):
    return lax.dot_general(a, b, (((0,), (0,)), ((), ())), preferred_element_type=F32)


def iota(shape, dim):
    return lax.broadcasted_iota(jnp.int32, shape, dim)


def ones(cond, dtype=BF):
    return jnp.where(cond, 1.0, 0.0).astype(dtype)


def slot_codes(ids_t, parity, n_dst, none):
    picks, tok = ids_t.shape
    expert = 2 * iota((n_dst, tok), 0) + parity
    named = jnp.zeros((n_dst, tok), F32)
    for k in range(picks):
        named = named + ones(ids_t[k : k + 1, :] == expert, F32)
    earlier = ones(iota((tok, tok), 0) < iota((tok, tok), 1))
    place = dot(named.astype(BF), earlier)
    code = jnp.where(named > 0, place, none)
    spread = ones((iota((n_dst * ROWS, n_dst), 0) // ROWS) == iota((n_dst * ROWS, n_dst), 1))
    return dot(spread, code.astype(BF)), spread


def selections(code):
    row = iota(code.shape, 0) % ROWS
    slot = row.astype(F32)
    low = row < 4
    return (
        code == slot,
        code == slot + 8.0,
        (code == slot + 16.0) & low,
        (code == slot + 12.0) & jnp.logical_not(low),
    )


def route_kernel(n_dst, place_ref, ids_ref, tok_hbm, kv_ref, out_ref, tok_ref, sem):
    quarter = tok_ref.shape[1]
    half = quarter // 2
    cols = pl.ds(pl.multiple_of(place_ref[0] * quarter, quarter), quarter)
    copy = pltpu.make_async_copy(tok_hbm.at[:, cols], tok_ref, sem)
    copy.start()
    code, _ = slot_codes(ids_ref[...], place_ref[1], n_dst, 200.0)
    first, second, low, high = selections(code)
    n, t = code.shape
    row, col = iota((n, t), 0), iota((n, t), 1)
    piece = (col == (row % ROWS) * PAGE + row // ROWS) & (row % ROWS < t // PAGE)
    out_ref[:, 2 * quarter + half :] = dot(ones(piece), kv_ref[...]).astype(BF)
    copy.wait()
    tok = tok_ref[...]
    out_ref[:, :quarter] = dot(ones(first), tok).astype(BF)
    out_ref[:, quarter : 2 * quarter] = dot(ones(second), tok).astype(BF)
    out_ref[:, 2 * quarter : 2 * quarter + half] = (
        dot(ones(low), tok[:, :half]) + dot(ones(high), tok[:, half:])
    ).astype(BF)


def weights_kernel(place_ref, wg_ref, wu_ref, wd_ref, *refs):
    outs, sems = refs[:-1], refs[-1]
    y, core = place_ref[0], place_ref[1]
    quarter = outs[2].shape[1]
    copies = []
    for i, (by, other) in enumerate(MOVES):
        to_y = lax.rem(y + by, 4)
        to_core = 1 - core if other else core
        cols = pl.ds(pl.multiple_of(to_y * quarter, quarter), quarter)
        copies.append((wd_ref.at[to_core, :, cols], outs[2 + i]))
    copies += [(wg_ref.at[1 - core], outs[0]), (wu_ref.at[1 - core], outs[1])]
    copies = [pltpu.make_async_copy(a, b, sems.at[i]) for i, (a, b) in enumerate(copies)]
    for c in copies:
        c.start()
    for c in copies:
        c.wait()


def unpack_kernel(in_ref, slots_ref, p_ref, q_ref, kv_ref):
    n = in_ref.shape[0]
    quarter = p_ref.shape[1]
    half = quarter // 2
    p_ref[...] = in_ref[:, :quarter]
    q_ref[:n] = in_ref[:, quarter : 2 * quarter]
    m = n // 2
    row, col = iota((m, n), 0), iota((m, n), 1)
    at = (row // 4) * ROWS + row % 4
    mixed = in_ref[:, 2 * quarter : 2 * quarter + half]
    q_ref[n:, :half] = dot(ones(col == at), mixed).astype(BF)
    q_ref[n:, half:] = dot(ones(col == at + 4), mixed).astype(BF)
    pages = slots_ref.shape[1]
    row, col = iota((pages, n), 0), iota((pages, n), 1)
    held = col % ROWS < 4
    spread = ones(held & (row == (col // ROWS) * 4 + col % ROWS))
    slots = jnp.broadcast_to(slots_ref[...].astype(F32), (8, pages)).astype(BF)
    slots = jnp.where(held[0:1], dot(slots, spread)[0:1], -2.0)
    row = iota((n, n), 0)
    wanted = jnp.where(row % ROWS < 4, (row // ROWS) * 4 + row % ROWS, -1).astype(F32)
    kv_ref[...] = dot(ones(slots == wanted), in_ref[:, 2 * quarter + half :]).astype(BF)


def up_kernel(
    place_ref, own_ref, left_ref, right_ref, far_ref, wg_ref, wg2_ref, wu_ref, wu2_ref, s_ref, out_ref, g_ref, u_ref
):
    k = pl.program_id(0)

    def step(x_ref, first):
        x = x_ref[...]
        g = dot_nt(x, jnp.concatenate([wg_ref[0], wg2_ref[...]], axis=0))
        u = dot_nt(x, jnp.concatenate([wu_ref[0], wu2_ref[...]], axis=0))
        if first:
            g_ref[...], u_ref[...] = g, u
        else:
            g_ref[...] += g
            u_ref[...] += u

    for i, ref in enumerate((own_ref, left_ref, right_ref, far_ref)):
        pl.when(k == i)(functools.partial(step, ref, i == 0))

    @pl.when(k == 3)
    def _():
        g = g_ref[...] * s_ref[0:1, :]
        u = u_ref[...] * s_ref[1:2, :]
        out_ref[...] = (g / (1.0 + jnp.exp(-g)) * u).astype(BF)


def down_sum(refs):
    acc = None
    for i in range(4):
        w = jnp.concatenate([refs[4 + 2 * i][...], refs[5 + 2 * i][...]], axis=0)
        part = dot(refs[i][...], w)
        acc = part if acc is None else acc + part
    return (acc * refs[12][0]).astype(BF)


def down_kernel(place_ref, *refs):
    refs[13][...] = down_sum(refs)


def down_pack_kernel(place_ref, *refs):
    y = down_sum(refs)
    kv_ref, out_ref = refs[13:]
    n, quarter = kv_ref.shape[0], y.shape[1]
    half = quarter // 2
    out_ref[:, :quarter] = y[:n]
    rest = y[n:]
    m = n // 2
    row, col = iota((n, m), 0), iota((n, m), 1)
    hit = col == (row // ROWS) * 4 + row % 4
    low = row % ROWS < 4
    out_ref[:, quarter : quarter + half] = (
        dot(ones(hit & low), rest[:, :half]) + dot(ones(hit & jnp.logical_not(low)), rest[:, half:])
    ).astype(BF)
    out_ref[:, quarter + half :] = kv_ref[...]


def combine_kernel(n_dst, place_ref, ids_ref, gates_ref, p_ref, q_ref, keep_ref, send_ref, kv_ref):
    parity = place_ref[1]
    ids, gates = ids_ref[...], gates_ref[...]
    code, spread = slot_codes(ids, parity, n_dst, 200.0)
    picks, tok = ids.shape
    expert = 2 * iota((n_dst, tok), 0) + parity
    gate = jnp.zeros((n_dst, tok), F32)
    for k in range(picks):
        gate = gate + jnp.where(ids[k : k + 1, :] == expert, gates[k : k + 1, :], 0.0)
    top = gate.astype(BF)
    rest = (gate - top.astype(F32)).astype(BF)
    top, rest = dot(spread, top), dot(spread, rest)
    first, second, low, high = selections(code)

    def mix(where, rows):
        return dot_tn(jnp.where(where, top, 0.0).astype(BF), rows) + dot_tn(
            jnp.where(where, rest, 0.0).astype(BF), rows
        )

    quarter = p_ref.shape[1]
    half = quarter // 2
    mixed = q_ref[:, quarter : quarter + half]
    sums = []
    for where, lo in ((low, 0), (high, half)):
        cols = slice(lo, lo + half)
        sums.append(mix(first, p_ref[:, cols]) + mix(second, q_ref[:, cols]) + mix(where, mixed))
    even = parity == 0
    keep_ref[...] = jnp.where(even, sums[0], sums[1])
    send_ref[...] = jnp.where(even, sums[1], sums[0])
    n = q_ref.shape[0]
    row, col = iota((tok, n), 0), iota((tok, n), 1)
    kv_ref[...] = dot(ones(col == (row % PAGE) * ROWS + row // PAGE), q_ref[:, quarter + half :]).astype(BF)


def sds(*shape, dtype=BF):
    return jax.ShapeDtypeStruct(shape, dtype)


def whole(*shape):
    return pl.BlockSpec(shape, lambda *a: (0,) * len(shape))


PARAMS = pltpu.CompilerParams(vmem_limit_bytes=62 * 1024 * 1024)


def on_device(
    tokens, expert_ids, gates, w_gate, w_up, w_down, gate_scale, up_scale, down_scale, kv_rows, page_slots
):
    y, core = lax.axis_index("y"), lax.axis_index("core")
    n_dp = lax.axis_size("z") * lax.axis_size("x")
    n_y, n_core = lax.axis_size("y"), lax.axis_size("core")
    tok, width = tokens.shape
    quarter = width // n_y
    half = quarter // 2
    experts, hid = w_gate.shape[:2]
    kv_cols = kv_rows.shape[1]
    rows = n_dp * ROWS
    place = jnp.stack([y, core]).astype(jnp.int32)
    ids_t, gates_t = expert_ids.T, gates.T
    picks = ids_t.shape[0]

    payload = 2 * quarter + half + kv_cols
    hbm = pl.BlockSpec(memory_space=pltpu.HBM)
    vmem = pl.BlockSpec(memory_space=pltpu.VMEM)
    smem = pl.BlockSpec(memory_space=pltpu.SMEM)
    with jax.named_scope("route"):
        outgoing = pl.pallas_call(
            functools.partial(route_kernel, n_dp),
            in_specs=[smem, vmem, hbm, vmem],
            out_specs=vmem,
            out_shape=sds(rows, payload),
            scratch_shapes=[pltpu.VMEM((tok, quarter), BF), pltpu.SemaphoreType.DMA],
            compiler_params=PARAMS,
        )(place, ids_t, tokens, kv_rows)

    def exchange(v):
        return lax.all_to_all(v.reshape(n_dp, ROWS, v.shape[-1]), DP, 0, 0, tiled=True).reshape(v.shape)

    with jax.named_scope("dispatch"):
        arrived = exchange(outgoing)

    swap = [(0, 1), (1, 0)]
    with jax.named_scope("weights"):
        parts = pl.pallas_call(
            weights_kernel,
            in_specs=[smem, hbm, hbm, hbm],
            out_specs=[vmem] * 10,
            out_shape=[sds(hid, width)] * 2 + [sds(hid, quarter)] * 8,
            scratch_shapes=[pltpu.SemaphoreType.DMA((10,))],
            compiler_params=PARAMS,
        )(place, w_gate, w_up, w_down)
        wd = [parts[2]]
        for (by, other), v in zip(MOVES[1:], parts[3:]):
            pairs = [
                (i * n_core + c, (i + by) % n_y * n_core + (1 - c if other else c))
                for i in range(n_y)
                for c in range(n_core)
            ]
            wd.append(lax.ppermute(v, ("y", "core"), pairs))
        wg2 = lax.ppermute(parts[0], "core", swap)
        wu2 = lax.ppermute(parts[1], "core", swap)
        both = jnp.stack([gate_scale, up_scale])
        own = lax.dynamic_index_in_dim(both, core, 1, keepdims=False)
        other = lax.ppermute(lax.dynamic_index_in_dim(both, 1 - core, 1, keepdims=False), "core", swap)
        scales = jnp.concatenate([own, other], axis=1)

    def after(v, *others):
        return lax.optimization_barrier((v, *others))[0]

    with jax.named_scope("unpack"):
        x_p, x_q, kv_q = pl.pallas_call(
            unpack_kernel,
            out_shape=[sds(rows, quarter), sds(rows + rows // 2, quarter), sds(rows, kv_cols)],
            compiler_params=PARAMS,
        )(after(arrived, *wd, wg2, wu2, scales), page_slots.reshape(1, -1))

    def shift(v, by):
        return lax.ppermute(v, "y", [(i, (i + by) % n_y) for i in range(n_y)])

    with jax.named_scope("rows"):
        p_left, p_right = shift(x_p, 1), shift(x_p, -1)
        x_q = after(x_q, p_left, p_right)
        p_far = shift(p_left, 1)
        q_left, q_right = shift(x_q, 1), shift(x_q, -1)
        q_far = shift(q_right, -1)

    def piece(k, p):
        return (p[0] + jnp.where(k == 0, 0, jnp.where(k == 1, 3, jnp.where(k == 2, 1, 2)))) % 4

    units = n_core * hid

    def up(pieces):
        r = pieces[0].shape[0]
        return pl.pallas_call(
            up_kernel,
            grid_spec=pltpu.PrefetchScalarGridSpec(
                num_scalar_prefetch=1,
                grid=(4,),
                in_specs=[whole(r, quarter)] * 4
                + [
                    pl.BlockSpec((1, hid, quarter), lambda k, p: (p[1], 0, piece(k, p))),
                    pl.BlockSpec((hid, quarter), lambda k, p: (0, piece(k, p))),
                ]
                * 2
                + [whole(2, units)],
                out_specs=whole(r, units),
                scratch_shapes=[pltpu.VMEM((r, units), F32)] * 2,
            ),
            out_shape=sds(r, units),
            compiler_params=PARAMS,
        )(place, *pieces, w_gate, wg2, w_up, wu2, scales)

    def down(pieces, kv=None):
        r = pieces[0].shape[0]
        shape = (r, quarter) if kv is None else (rows, quarter + half + kv_cols)
        return pl.pallas_call(
            down_kernel if kv is None else down_pack_kernel,
            grid_spec=pltpu.PrefetchScalarGridSpec(
                num_scalar_prefetch=1,
                grid=(1,),
                in_specs=[whole(r, units)] * 4
                + [whole(hid, quarter)] * 8
                + [pl.BlockSpec((1, 1, quarter), lambda k, p: (p[1], 0, p[0]))]
                + ([] if kv is None else [whole(rows, kv_cols)]),
                out_specs=whole(*shape),
            ),
            out_shape=sds(*shape),
            compiler_params=PARAMS,
        )(place, *pieces, *wd, down_scale.reshape(experts, 1, width), *([] if kv is None else [kv]))

    def hidden_pieces(h):
        return h, shift(h, 1), shift(h, -1), shift(h, 2)

    out = []
    for pieces, kv in (((x_p, p_left, p_right, p_far), None), ((x_q, q_left, q_right, q_far), kv_q)):
        with jax.named_scope("up"):
            h = up(pieces)
        with jax.named_scope("down"):
            v = down(hidden_pieces(h), kv)
        with jax.named_scope("back"):
            out.append(exchange(v))

    with jax.named_scope("combine"):
        keep, send, kv_cache = pl.pallas_call(
            functools.partial(combine_kernel, n_dp),
            in_specs=[pl.BlockSpec(memory_space=pltpu.SMEM)] + [pl.BlockSpec(memory_space=pltpu.VMEM)] * 4,
            out_shape=[sds(tok, half, dtype=F32), sds(tok, half, dtype=F32), sds(tok, kv_cols)],
            compiler_params=PARAMS,
        )(place, ids_t, gates_t, *out)
        moe_out = (keep + lax.ppermute(send, "core", [(0, 1), (1, 0)])).astype(BF)
    return moe_out, kv_cache.reshape(tok // PAGE, PAGE, kv_cols)


def solution(mesh):
    shape = mesh.devices.shape
    n_z, n_x, n_y = 8, 4, 4
    fine = Mesh(np.asarray(mesh.devices).reshape(n_z, n_x, n_y, shape[1] // n_y), ("z", "x", "y", "core"))
    group = ("y", "core")
    placed = (
        P(DP, None),
        P(DP, None),
        P(DP, None),
        P(DP, group, None),
        P(DP, group, None),
        P(DP, group, None),
        P(DP, group),
        P(DP, group),
        P(DP, None),
        P(DP, group),
        P(),
    )
    return jax.shard_map(
        on_device,
        mesh=fine,
        in_specs=placed,
        out_specs=(P(DP, group), P(DP, None, group)),
        check_vma=False,
    )
```

```python
import functools

import jax
import jax.numpy as jnp
import numpy as np
from jax import lax
from jax.experimental import pallas as pl
from jax.experimental.pallas import tpu as pltpu
from jax.sharding import Mesh
from jax.sharding import PartitionSpec as P

BF = jnp.bfloat16
F32 = jnp.float32
PAGE = 32
ROWS = 8
DP = ("z", "x")
MOVES = ((0, False), (0, True), (1, False), (1, True), (3, False), (3, True), (2, False), (2, True))


def dot(a, b):
    return lax.dot_general(a, b, (((1,), (0,)), ((), ())), preferred_element_type=F32)


def dot_nt(a, b):
    return lax.dot_general(a, b, (((1,), (1,)), ((), ())), preferred_element_type=F32)


def dot_tn(a, b):
    return lax.dot_general(a, b, (((0,), (0,)), ((), ())), preferred_element_type=F32)


def iota(shape, dim):
    return lax.broadcasted_iota(jnp.int32, shape, dim)


def ones(cond, dtype=BF):
    return jnp.where(cond, 1.0, 0.0).astype(dtype)


def slot_codes(ids_t, parity, n_dst, none):
    picks, tok = ids_t.shape
    expert = 2 * iota((n_dst, tok), 0) + parity
    named = jnp.zeros((n_dst, tok), F32)
    for k in range(picks):
        named = named + ones(ids_t[k : k + 1, :] == expert, F32)
    earlier = ones(iota((tok, tok), 0) < iota((tok, tok), 1))
    place = dot(named.astype(BF), earlier)
    code = jnp.where(named > 0, place, none)
    spread = ones((iota((n_dst * ROWS, n_dst), 0) // ROWS) == iota((n_dst * ROWS, n_dst), 1))
    return dot(spread, code.astype(BF)), spread


def selections(code):
    row = iota(code.shape, 0) % ROWS
    slot = row.astype(F32)
    low = row < 4
    return (
        code == slot,
        code == slot + 8.0,
        (code == slot + 16.0) & low,
        (code == slot + 12.0) & jnp.logical_not(low),
    )


def route_kernel(n_dst, place_ref, ids_ref, tok_hbm, kv_ref, wg_hbm, wu_hbm, wd_hbm, out_ref, g_ref, u_ref, *refs):
    cuts, (tok_ref, sems) = refs[:-2], refs[-2:]
    quarter = tok_ref.shape[1]
    half = quarter // 2
    y, core = place_ref[0], place_ref[1]
    cols = pl.ds(pl.multiple_of(y * quarter, quarter), quarter)
    copies = [(tok_hbm.at[:, cols], tok_ref)]
    for (by, other), cut in zip(MOVES, cuts):
        cols = pl.ds(pl.multiple_of(lax.rem(y + by, 4) * quarter, quarter), quarter)
        copies.append((wd_hbm.at[1 - core if other else core, :, cols], cut))
    sibling = pl.ds(1 - core, 1)
    copies += [(wg_hbm.at[sibling], g_ref), (wu_hbm.at[sibling], u_ref)]
    copies = [pltpu.make_async_copy(a, b, sems.at[i]) for i, (a, b) in enumerate(copies)]
    for c in copies:
        c.start()
    code, _ = slot_codes(ids_ref[...], place_ref[1], n_dst, 200.0)
    first, second, low, high = selections(code)
    n, t = code.shape
    row, col = iota((n, t), 0), iota((n, t), 1)
    piece = (col == (row % ROWS) * PAGE + row // ROWS) & (row % ROWS < t // PAGE)
    out_ref[:, 2 * quarter + half :] = dot(ones(piece), kv_ref[...]).astype(BF)
    copies[0].wait()
    tok = tok_ref[...]
    out_ref[:, :quarter] = dot(ones(first), tok).astype(BF)
    out_ref[:, quarter : 2 * quarter] = dot(ones(second), tok).astype(BF)
    out_ref[:, 2 * quarter : 2 * quarter + half] = (
        dot(ones(low), tok[:, :half]) + dot(ones(high), tok[:, half:])
    ).astype(BF)
    for c in copies[1:]:
        c.wait()


def unpack_kernel(in_ref, slots_ref, p_ref, q_ref, kv_ref):
    n = in_ref.shape[0]
    quarter = q_ref.shape[1]
    half = quarter // 2
    p_ref[...] = in_ref[:, :quarter]
    q_ref[:n] = in_ref[:, quarter : 2 * quarter]
    m = n // 2
    row, col = iota((m, n), 0), iota((m, n), 1)
    at = (row // 4) * ROWS + row % 4
    mixed = in_ref[:, 2 * quarter : 2 * quarter + half]
    q_ref[n:, :half] = dot(ones(col == at), mixed).astype(BF)
    q_ref[n:, half:] = dot(ones(col == at + 4), mixed).astype(BF)
    pages = slots_ref.shape[1]
    row, col = iota((pages, n), 0), iota((pages, n), 1)
    held = col % ROWS < 4
    spread = ones(held & (row == (col // ROWS) * 4 + col % ROWS))
    slots = jnp.broadcast_to(slots_ref[...].astype(F32), (8, pages)).astype(BF)
    slots = jnp.where(held[0:1], dot(slots, spread)[0:1], -2.0)
    row = iota((n, n), 0)
    wanted = jnp.where(row % ROWS < 4, (row // ROWS) * 4 + row % ROWS, -1).astype(F32)
    kv_ref[...] = dot(ones(slots == wanted), in_ref[:, 2 * quarter + half :]).astype(BF)


def gated(both, s_ref):
    n = s_ref.shape[1]
    g, u = both[:, :n] * s_ref[0:1, :], both[:, n:] * s_ref[1:2, :]
    return (g / (1.0 + jnp.exp(-g)) * u).astype(BF)


def up_step(acc_ref, x_ref, w_refs, first):
    w = jnp.concatenate([ref[0] for ref in w_refs], axis=0)
    both = dot_nt(x_ref[...], w)
    if first:
        acc_ref[...] = both
    else:
        acc_ref[...] += both


def up_kernel(place_ref, *refs):
    w_refs, s_ref, out_ref, acc_ref = refs[4:8], refs[8], refs[9], refs[10]
    k = pl.program_id(0)
    for i in range(4):
        pl.when(k == i)(functools.partial(up_step, acc_ref, refs[i], w_refs, i == 0))

    @pl.when(k == 3)
    def _():
        out_ref[...] = gated(acc_ref[...], s_ref)


def up_first_kernel(place_ref, *refs):
    k = pl.program_id(0)
    for i in range(2):
        pl.when(k == i)(functools.partial(up_step, refs[6], refs[i], refs[2:6], i == 0))


def up_last_kernel(place_ref, *refs):
    w_refs, part_ref, s_ref, out_ref, acc_ref = refs[2:6], refs[6], refs[7], refs[8], refs[9]
    k = pl.program_id(0)
    for i in range(2):
        pl.when(k == i)(functools.partial(up_step, acc_ref, refs[i], w_refs, i == 0))

    @pl.when(k == 1)
    def _():
        out_ref[...] = gated(acc_ref[...] + part_ref[...], s_ref)


def down_sum(h_refs, w_refs):
    acc = None
    for i, h_ref in enumerate(h_refs):
        w = jnp.concatenate([w_refs[2 * i][...], w_refs[2 * i + 1][...]], axis=0)
        part = dot(h_ref[...], w)
        acc = part if acc is None else acc + part
    return acc


def down_kernel(place_ref, *refs):
    refs[13][...] = (down_sum(refs[:4], refs[4:12]) * refs[12][0]).astype(BF)


def down_first_kernel(h_ref, same_ref, cross_ref, out_ref):
    out_ref[...] = down_sum((h_ref,), (same_ref, cross_ref))


def down_last_kernel(place_ref, *refs):
    acc_ref, s_ref, kv_ref, out_ref = refs[9:]
    y = ((acc_ref[...] + down_sum(refs[:3], refs[3:9])) * s_ref[0]).astype(BF)
    n, quarter = kv_ref.shape[0], y.shape[1]
    half = quarter // 2
    out_ref[:, :quarter] = y[:n]
    rest = y[n:]
    m = n // 2
    row, col = iota((n, m), 0), iota((n, m), 1)
    hit = col == (row // ROWS) * 4 + row % 4
    low = row % ROWS < 4
    out_ref[:, quarter : quarter + half] = (
        dot(ones(hit & low), rest[:, :half]) + dot(ones(hit & jnp.logical_not(low)), rest[:, half:])
    ).astype(BF)
    out_ref[:, quarter + half :] = kv_ref[...]


def combine_kernel(n_dst, place_ref, ids_ref, gates_ref, p_ref, q_ref, keep_ref, send_ref, kv_ref):
    parity = place_ref[1]
    ids, gates = ids_ref[...], gates_ref[...]
    code, spread = slot_codes(ids, parity, n_dst, 200.0)
    picks, tok = ids.shape
    expert = 2 * iota((n_dst, tok), 0) + parity
    gate = jnp.zeros((n_dst, tok), F32)
    for k in range(picks):
        gate = gate + jnp.where(ids[k : k + 1, :] == expert, gates[k : k + 1, :], 0.0)
    top = gate.astype(BF)
    rest = (gate - top.astype(F32)).astype(BF)
    top, rest = dot(spread, top), dot(spread, rest)
    first, second, low, high = selections(code)

    def mix(where, rows):
        return dot_tn(jnp.where(where, top, 0.0).astype(BF), rows) + dot_tn(
            jnp.where(where, rest, 0.0).astype(BF), rows
        )

    quarter = p_ref.shape[1]
    half = quarter // 2
    mixed = q_ref[:, quarter : quarter + half]
    sums = []
    for where, lo in ((low, 0), (high, half)):
        cols = slice(lo, lo + half)
        sums.append(mix(first, p_ref[:, cols]) + mix(second, q_ref[:, cols]) + mix(where, mixed))
    even = parity == 0
    keep_ref[...] = jnp.where(even, sums[0], sums[1])
    send_ref[...] = jnp.where(even, sums[1], sums[0])
    n = q_ref.shape[0]
    row, col = iota((tok, n), 0), iota((tok, n), 1)
    kv_ref[...] = dot(ones(col == (row % PAGE) * ROWS + row // PAGE), q_ref[:, quarter + half :]).astype(BF)


def sds(*shape, dtype=BF):
    return jax.ShapeDtypeStruct(shape, dtype)


def whole(*shape):
    return pl.BlockSpec(shape, lambda *a: (0,) * len(shape))


CHEAP = pl.CostEstimate(flops=1000, bytes_accessed=1000, transcendentals=0)
PARAMS = pltpu.CompilerParams(vmem_limit_bytes=62 * 1024 * 1024)


def on_device(
    tokens, expert_ids, gates, w_gate, w_up, w_down, gate_scale, up_scale, down_scale, kv_rows, page_slots
):
    y, core = lax.axis_index("y"), lax.axis_index("core")
    n_dp = lax.axis_size("z") * lax.axis_size("x")
    n_y, n_core = lax.axis_size("y"), lax.axis_size("core")
    tok, width = tokens.shape
    quarter = width // n_y
    half = quarter // 2
    experts, hid = w_gate.shape[:2]
    kv_cols = kv_rows.shape[1]
    rows = n_dp * ROWS
    place = jnp.stack([y, core]).astype(jnp.int32)
    ids_t, gates_t = expert_ids.T, gates.T
    picks = ids_t.shape[0]

    payload = quarter + half + kv_cols
    hbm = pl.BlockSpec(memory_space=pltpu.HBM)
    vmem = pl.BlockSpec(memory_space=pltpu.VMEM)
    smem = pl.BlockSpec(memory_space=pltpu.SMEM)
    swap = [(0, 1), (1, 0)]

    def after(v, *others):
        return lax.optimization_barrier((v, *others))[0]

    with jax.named_scope("route"):
        outgoing, other_g, other_u, *cuts = pl.pallas_call(
            functools.partial(route_kernel, n_dp),
            in_specs=[smem, vmem, hbm, vmem, hbm, hbm, hbm],
            out_specs=[vmem] * 11,
            out_shape=[sds(rows, quarter + payload)] + [sds(1, hid, width)] * 2 + [sds(hid, quarter)] * 8,
            scratch_shapes=[pltpu.VMEM((tok, quarter), BF), pltpu.SemaphoreType.DMA((11,))],
            compiler_params=PARAMS,
            cost_estimate=CHEAP,
        )(place, ids_t, tokens, kv_rows, w_gate, w_up, w_down)
        wd = [cuts[0]]
        for (by, other), v in zip(MOVES[1:], cuts[1:]):
            pairs = [
                (i * n_core + c, (i + by) % n_y * n_core + (1 - c if other else c))
                for i in range(n_y)
                for c in range(n_core)
            ]
            wd.append(lax.ppermute(v, ("y", "core"), pairs))

    def exchange(v):
        return lax.all_to_all(v.reshape(n_dp, ROWS, v.shape[-1]), DP, 0, 0, tiled=True).reshape(v.shape)

    with jax.named_scope("dispatch"):
        arrived = exchange(outgoing)

    with jax.named_scope("scales"):
        both = jnp.stack([gate_scale, up_scale])
        own = lax.dynamic_index_in_dim(both, core, 1, keepdims=False)
        other = lax.ppermute(lax.dynamic_index_in_dim(both, 1 - core, 1, keepdims=False), "core", swap)
        scales = jnp.concatenate([own, other], axis=1)

    with jax.named_scope("unpack"):
        x_p, x_q, kv_q = pl.pallas_call(
            unpack_kernel,
            out_shape=[sds(rows, quarter), sds(rows + rows // 2, quarter), sds(rows, kv_cols)],
            compiler_params=PARAMS,
            cost_estimate=CHEAP,
        )(after(arrived, *wd, scales), page_slots.reshape(1, -1))

    def shift(v, by):
        return lax.ppermute(v, "y", [(i, (i + by) % n_y) for i in range(n_y)])

    with jax.named_scope("rows"):
        p_left, p_right = shift(x_p, 1), shift(x_p, -1)
        p_far = shift(p_left, 1)
        q_right = shift(after(x_q, p_right), -1)
        q_left = shift(after(x_q, p_far), 1)
        q_far = shift(q_right, -1)

    with jax.named_scope("swap"):
        w2 = [lax.ppermute(w, "core", swap) for w in (other_g, other_u)]

    units = n_core * hid

    def columns(k, p, steps):
        by = steps[0]
        for i, s in enumerate(steps[1:], 1):
            by = jnp.where(k == i, s, by)
        return lax.rem(p[0] + by, n_y)

    def weight_specs(*steps):
        def own():
            return pl.BlockSpec((1, hid, quarter), lambda k, p: (p[1], 0, columns(k, p, steps)))

        def other():
            return pl.BlockSpec((1, hid, quarter), lambda k, p: (0, 0, columns(k, p, steps)))

        return [own(), other(), own(), other()]

    def call(kernel, steps, in_specs, out_specs, out_shape, scratch=()):
        return pl.pallas_call(
            kernel,
            grid_spec=pltpu.PrefetchScalarGridSpec(
                num_scalar_prefetch=1,
                grid=(steps,),
                in_specs=in_specs,
                out_specs=out_specs,
                scratch_shapes=list(scratch),
            ),
            out_shape=out_shape,
            compiler_params=PARAMS,
            cost_estimate=CHEAP,
        )

    weights = (w_gate, w2[0], w_up, w2[1])
    channel = pl.BlockSpec((1, 1, quarter), lambda k, p: (p[1], 0, p[0]))
    down_scale = down_scale.reshape(experts, 1, width)

    def acc(r):
        return [pltpu.VMEM((r, 2 * units), F32)]

    with jax.named_scope("up"):
        r = rows
        h_p = call(
            up_kernel,
            4,
            [whole(r, quarter)] * 4 + weight_specs(0, 3, 1, 2) + [whole(2, units)],
            whole(r, units),
            sds(r, units),
            acc(r),
        )(place, x_p, p_left, p_right, p_far, *weights, scales)

    with jax.named_scope("up"):
        r = rows + rows // 2
        both_q = call(
            up_first_kernel,
            2,
            [whole(r, quarter)] * 2 + weight_specs(0, 1),
            whole(r, 2 * units),
            sds(r, 2 * units, dtype=F32),
        )(place, x_q, q_right, *weights)
    with jax.named_scope("down"):
        near = [shift(h_p, 1), shift(h_p, -1), shift(h_p, 2)]
        near[2] = after(near[2], both_q)
        r = rows
        v_p = call(
            down_kernel,
            1,
            [whole(r, units)] * 4 + [whole(hid, quarter)] * 8 + [channel],
            whole(r, quarter),
            sds(r, quarter),
        )(place, h_p, *near, *wd, down_scale)
        back_p = exchange(v_p)

    with jax.named_scope("up"):
        r = rows + rows // 2
        h_q = call(
            up_last_kernel,
            2,
            [whole(r, quarter)] * 2 + weight_specs(3, 2) + [whole(r, 2 * units), whole(2, units)],
            whole(r, units),
            sds(r, units),
            acc(r),
        )(place, q_left, q_far, *weights, both_q, scales)

    with jax.named_scope("down"):
        near = [shift(h_q, 1), shift(h_q, -1), shift(h_q, 2)]
        part = pl.pallas_call(
            down_first_kernel,
            out_shape=sds(r, quarter, dtype=F32),
            compiler_params=PARAMS,
            cost_estimate=CHEAP,
        )(h_q, *wd[:2])
        v_q = call(
            down_last_kernel,
            1,
            [whole(r, units)] * 3
            + [whole(hid, quarter)] * 6
            + [whole(r, quarter), channel, whole(rows, kv_cols)],
            whole(rows, payload),
            sds(rows, payload),
        )(place, *near, *wd[2:], part, down_scale, kv_q)
        back_q = exchange(v_q)

    with jax.named_scope("combine"):
        keep, send, kv_cache = pl.pallas_call(
            functools.partial(combine_kernel, n_dp),
            in_specs=[pl.BlockSpec(memory_space=pltpu.SMEM)] + [pl.BlockSpec(memory_space=pltpu.VMEM)] * 4,
            out_shape=[sds(tok, half, dtype=F32), sds(tok, half, dtype=F32), sds(tok, kv_cols)],
            compiler_params=PARAMS,
            cost_estimate=CHEAP,
        )(place, ids_t, gates_t, back_p, back_q)
        moe_out = (keep + lax.ppermute(send, "core", [(0, 1), (1, 0)])).astype(BF)
    return moe_out, kv_cache.reshape(tok // PAGE, PAGE, kv_cols)


def solution(mesh):
    shape = mesh.devices.shape
    n_z, n_x, n_y = 8, 4, 4
    fine = Mesh(np.asarray(mesh.devices).reshape(n_z, n_x, n_y, shape[1] // n_y), ("z", "x", "y", "core"))
    group = ("y", "core")
    placed = (
        P(DP, None),
        P(DP, None),
        P(DP, None),
        P(DP, group, None),
        P(DP, group, None),
        P(DP, group, None),
        P(DP, group),
        P(DP, group),
        P(DP, None),
        P(DP, group),
        P(),
    )
    return jax.shard_map(
        on_device,
        mesh=fine,
        in_specs=placed,
        out_specs=(P(DP, group), P(DP, None, group)),
        check_vma=False,
    )
```

```python
import functools

import jax
import jax.numpy as jnp
import numpy as np
from jax import lax
from jax.experimental import pallas as pl
from jax.experimental.pallas import tpu as pltpu
from jax.sharding import Mesh
from jax.sharding import PartitionSpec as P

BF = jnp.bfloat16
F32 = jnp.float32
PAGE = 32
ROWS = 8
DP = ("z", "x")
MOVES = ((0, False), (0, True), (1, False), (1, True), (3, False), (3, True), (2, False), (2, True))


def dot(a, b):
    return lax.dot_general(a, b, (((1,), (0,)), ((), ())), preferred_element_type=F32)


def dot_nt(a, b):
    return lax.dot_general(a, b, (((1,), (1,)), ((), ())), preferred_element_type=F32)


def dot_tn(a, b):
    return lax.dot_general(a, b, (((0,), (0,)), ((), ())), preferred_element_type=F32)


def iota(shape, dim):
    return lax.broadcasted_iota(jnp.int32, shape, dim)


def ones(cond, dtype=BF):
    return jnp.where(cond, 1.0, 0.0).astype(dtype)


def slot_codes(ids_t, parity, n_dst, none):
    picks, tok = ids_t.shape
    expert = 2 * iota((n_dst, tok), 0) + parity
    named = jnp.zeros((n_dst, tok), F32)
    for k in range(picks):
        named = named + ones(ids_t[k : k + 1, :] == expert, F32)
    earlier = ones(iota((tok, tok), 0) < iota((tok, tok), 1))
    place = dot(named.astype(BF), earlier)
    code = jnp.where(named > 0, place, none)
    spread = ones((iota((n_dst * ROWS, n_dst), 0) // ROWS) == iota((n_dst * ROWS, n_dst), 1))
    return dot(spread, code.astype(BF)), spread


def selections(code):
    row = iota(code.shape, 0) % ROWS
    slot = row.astype(F32)
    low = row < 4
    return (
        code == slot,
        code == slot + 8.0,
        (code == slot + 16.0) & low,
        (code == slot + 12.0) & jnp.logical_not(low),
    )


def route_kernel(n_dst, place_ref, ids_ref, tok_hbm, kv_ref, wd_hbm, out_ref, *refs):
    cuts, (tok_ref, sems) = refs[:-2], refs[-2:]
    quarter = tok_ref.shape[1]
    half = quarter // 2
    y, core = place_ref[0], place_ref[1]
    cols = pl.ds(pl.multiple_of(y * quarter, quarter), quarter)
    copies = [(tok_hbm.at[:, cols], tok_ref)]
    for (by, other), cut in zip(MOVES, cuts):
        cols = pl.ds(pl.multiple_of(lax.rem(y + by, 4) * quarter, quarter), quarter)
        copies.append((wd_hbm.at[1 - core if other else core, :, cols], cut))
    copies = [pltpu.make_async_copy(a, b, sems.at[i]) for i, (a, b) in enumerate(copies)]
    for c in copies:
        c.start()
    code, _ = slot_codes(ids_ref[...], place_ref[1], n_dst, 200.0)
    first, second, low, high = selections(code)
    n, t = code.shape
    row, col = iota((n, t), 0), iota((n, t), 1)
    piece = (col == (row % ROWS) * PAGE + row // ROWS) & (row % ROWS < t // PAGE)
    out_ref[:, 2 * quarter + half :] = dot(ones(piece), kv_ref[...]).astype(BF)
    copies[0].wait()
    tok = tok_ref[...]
    out_ref[:, :quarter] = dot(ones(first), tok).astype(BF)
    out_ref[:, quarter : 2 * quarter] = dot(ones(second), tok).astype(BF)
    out_ref[:, 2 * quarter : 2 * quarter + half] = (
        dot(ones(low), tok[:, :half]) + dot(ones(high), tok[:, half:])
    ).astype(BF)
    for c in copies[1:]:
        c.wait()


def other_kernel(place_ref, wg_ref, wu_ref, g_ref, u_ref, sems):
    sibling = pl.ds(1 - place_ref[1], 1)
    copies = [(wg_ref.at[sibling], g_ref), (wu_ref.at[sibling], u_ref)]
    copies = [pltpu.make_async_copy(a, b, sems.at[i]) for i, (a, b) in enumerate(copies)]
    for c in copies:
        c.start()
    for c in copies:
        c.wait()


def unpack_kernel(in_ref, slots_ref, p_ref, q_ref, kv_ref):
    n = in_ref.shape[0]
    quarter = q_ref.shape[1]
    half = quarter // 2
    p_ref[...] = in_ref[:, :quarter]
    q_ref[:n] = in_ref[:, quarter : 2 * quarter]
    m = n // 2
    row, col = iota((m, n), 0), iota((m, n), 1)
    at = (row // 4) * ROWS + row % 4
    mixed = in_ref[:, 2 * quarter : 2 * quarter + half]
    q_ref[n:, :half] = dot(ones(col == at), mixed).astype(BF)
    q_ref[n:, half:] = dot(ones(col == at + 4), mixed).astype(BF)
    pages = slots_ref.shape[1]
    row, col = iota((pages, n), 0), iota((pages, n), 1)
    held = col % ROWS < 4
    spread = ones(held & (row == (col // ROWS) * 4 + col % ROWS))
    slots = jnp.broadcast_to(slots_ref[...].astype(F32), (8, pages)).astype(BF)
    slots = jnp.where(held[0:1], dot(slots, spread)[0:1], -2.0)
    row = iota((n, n), 0)
    wanted = jnp.where(row % ROWS < 4, (row // ROWS) * 4 + row % ROWS, -1).astype(F32)
    kv_ref[...] = dot(ones(slots == wanted), in_ref[:, 2 * quarter + half :]).astype(BF)


def gated(both, s_ref):
    n = s_ref.shape[1]
    g, u = both[:, :n] * s_ref[0:1, :], both[:, n:] * s_ref[1:2, :]
    return (g / (1.0 + jnp.exp(-g)) * u).astype(BF)


def up_step(acc_ref, x_ref, w_refs, first):
    w = jnp.concatenate([ref[0] for ref in w_refs], axis=0)
    both = dot_nt(x_ref[...], w)
    if first:
        acc_ref[...] = both
    else:
        acc_ref[...] += both


def up_first_kernel(place_ref, *refs):
    *x_refs, w0, w1, w2, w3, acc_ref = refs
    k = pl.program_id(0)
    for i, x_ref in enumerate(x_refs):
        pl.when(k == i)(functools.partial(up_step, acc_ref, x_ref, (w0, w1, w2, w3), i == 0))


def up_last_kernel(place_ref, *refs):
    *x_refs, w0, w1, w2, w3, part_ref, s_ref, out_ref, acc_ref = refs
    k = pl.program_id(0)
    for i, x_ref in enumerate(x_refs):
        pl.when(k == i)(functools.partial(up_step, acc_ref, x_ref, (w0, w1, w2, w3), i == 0))

    @pl.when(k == len(x_refs) - 1)
    def _():
        out_ref[...] = gated(acc_ref[...] + part_ref[...], s_ref)


def down_sum(h_refs, w_refs):
    acc = None
    for i, h_ref in enumerate(h_refs):
        w = jnp.concatenate([w_refs[2 * i][...], w_refs[2 * i + 1][...]], axis=0)
        part = dot(h_ref[...], w)
        acc = part if acc is None else acc + part
    return acc


def down_kernel(place_ref, *refs):
    refs[13][...] = (down_sum(refs[:4], refs[4:12]) * refs[12][0]).astype(BF)


def down_first_kernel(h_ref, same_ref, cross_ref, out_ref):
    out_ref[...] = down_sum((h_ref,), (same_ref, cross_ref))


def down_last_kernel(place_ref, *refs):
    acc_ref, s_ref, kv_ref, out_ref = refs[9:]
    y = ((acc_ref[...] + down_sum(refs[:3], refs[3:9])) * s_ref[0]).astype(BF)
    n, quarter = kv_ref.shape[0], y.shape[1]
    half = quarter // 2
    out_ref[:, :quarter] = y[:n]
    rest = y[n:]
    m = n // 2
    row, col = iota((n, m), 0), iota((n, m), 1)
    hit = col == (row // ROWS) * 4 + row % 4
    low = row % ROWS < 4
    out_ref[:, quarter : quarter + half] = (
        dot(ones(hit & low), rest[:, :half]) + dot(ones(hit & jnp.logical_not(low)), rest[:, half:])
    ).astype(BF)
    out_ref[:, quarter + half :] = kv_ref[...]


def combine_first_kernel(n_dst, place_ref, ids_ref, gates_ref, in_ref, acc_ref, gates_out_ref):
    parity = place_ref[1]
    ids, gates = ids_ref[...], gates_ref[...]
    code, spread = slot_codes(ids, parity, n_dst, 200.0)
    picks, tok = ids.shape
    expert = 2 * iota((n_dst, tok), 0) + parity
    gate = jnp.zeros((n_dst, tok), F32)
    for k in range(picks):
        gate = gate + jnp.where(ids[k : k + 1, :] == expert, gates[k : k + 1, :], 0.0)
    top = gate.astype(BF)
    rest = (gate - top.astype(F32)).astype(BF)
    top, rest = dot(spread, top), dot(spread, rest)
    first, *others = selections(code)
    for i, where in enumerate(others):
        gates_out_ref[2 * i] = jnp.where(where, top, 0.0).astype(BF)
        gates_out_ref[2 * i + 1] = jnp.where(where, rest, 0.0).astype(BF)
    acc_ref[...] = dot_tn(jnp.where(first, top, 0.0).astype(BF), in_ref[...]) + dot_tn(
        jnp.where(first, rest, 0.0).astype(BF), in_ref[...]
    )


def combine_last_kernel(place_ref, g_ref, acc_ref, in_ref, keep_ref, send_ref, kv_ref):
    half = keep_ref.shape[1]
    quarter = 2 * half
    rows = in_ref[:, :quarter]
    mixed = in_ref[:, quarter : quarter + half]
    sums = acc_ref[...] + dot_tn(g_ref[0], rows) + dot_tn(g_ref[1], rows)
    low = sums[:, :half] + dot_tn(g_ref[2], mixed) + dot_tn(g_ref[3], mixed)
    high = sums[:, half:] + dot_tn(g_ref[4], mixed) + dot_tn(g_ref[5], mixed)
    even = place_ref[1] == 0
    keep_ref[...] = jnp.where(even, low, high)
    send_ref[...] = jnp.where(even, high, low)
    n, tok = in_ref.shape[0], keep_ref.shape[0]
    row, col = iota((tok, n), 0), iota((tok, n), 1)
    kv_ref[...] = dot(ones(col == (row % PAGE) * ROWS + row // PAGE), in_ref[:, quarter + half :]).astype(BF)


def sds(*shape, dtype=BF):
    return jax.ShapeDtypeStruct(shape, dtype)


def whole(*shape):
    return pl.BlockSpec(shape, lambda *a: (0,) * len(shape))


CHEAP = pl.CostEstimate(flops=1000, bytes_accessed=1000, transcendentals=0)
PARAMS = pltpu.CompilerParams(vmem_limit_bytes=62 * 1024 * 1024)
SMALL = pltpu.CompilerParams(vmem_limit_bytes=24 * 1024 * 1024)


def on_device(
    tokens, expert_ids, gates, w_gate, w_up, w_down, gate_scale, up_scale, down_scale, kv_rows, page_slots
):
    y, core = lax.axis_index("y"), lax.axis_index("core")
    n_dp = lax.axis_size("z") * lax.axis_size("x")
    n_y, n_core = lax.axis_size("y"), lax.axis_size("core")
    tok, width = tokens.shape
    quarter = width // n_y
    half = quarter // 2
    experts, hid = w_gate.shape[:2]
    kv_cols = kv_rows.shape[1]
    rows = n_dp * ROWS
    place = jnp.stack([y, core]).astype(jnp.int32)
    ids_t, gates_t = expert_ids.T, gates.T
    picks = ids_t.shape[0]

    payload = quarter + half + kv_cols
    hbm = pl.BlockSpec(memory_space=pltpu.HBM)
    vmem = pl.BlockSpec(memory_space=pltpu.VMEM)
    smem = pl.BlockSpec(memory_space=pltpu.SMEM)
    swap = [(0, 1), (1, 0)]

    def after(v, *others):
        return lax.optimization_barrier((v, *others))[0]

    with jax.named_scope("route"):
        outgoing, *cuts = pl.pallas_call(
            functools.partial(route_kernel, n_dp),
            in_specs=[smem, vmem, hbm, vmem, hbm],
            out_specs=[vmem] * 9,
            out_shape=[sds(rows, quarter + payload)] + [sds(hid, quarter)] * 8,
            scratch_shapes=[pltpu.VMEM((tok, quarter), BF), pltpu.SemaphoreType.DMA((9,))],
            compiler_params=PARAMS,
            cost_estimate=CHEAP,
        )(place, ids_t, tokens, kv_rows, w_down)
        other_g, other_u = pl.pallas_call(
            other_kernel,
            in_specs=[smem, hbm, hbm],
            out_specs=[vmem] * 2,
            out_shape=[sds(1, hid, width)] * 2,
            scratch_shapes=[pltpu.SemaphoreType.DMA((2,))],
            compiler_params=PARAMS,
            cost_estimate=CHEAP,
        )(place, after(w_gate, outgoing), w_up)
        wd = [cuts[0]]
        for (by, other), v in zip(MOVES[1:], cuts[1:]):
            pairs = [
                (i * n_core + c, (i + by) % n_y * n_core + (1 - c if other else c))
                for i in range(n_y)
                for c in range(n_core)
            ]
            if len(wd) == 7:
                v = after(v, other_g)
            wd.append(lax.ppermute(v, ("y", "core"), pairs))

    def exchange(v):
        return lax.all_to_all(v.reshape(n_dp, ROWS, v.shape[-1]), DP, 0, 0, tiled=True).reshape(v.shape)

    with jax.named_scope("dispatch"):
        arrived = exchange(outgoing)

    with jax.named_scope("scales"):
        both = jnp.stack([gate_scale, up_scale])
        own = lax.dynamic_index_in_dim(both, core, 1, keepdims=False)
        other = lax.ppermute(lax.dynamic_index_in_dim(both, 1 - core, 1, keepdims=False), "core", swap)
        scales = jnp.concatenate([own, other], axis=1)

    with jax.named_scope("unpack"):
        x_p, x_q, kv_q = pl.pallas_call(
            unpack_kernel,
            out_shape=[sds(rows, quarter), sds(rows + rows // 2, quarter), sds(rows, kv_cols)],
            compiler_params=PARAMS,
            cost_estimate=CHEAP,
        )(after(arrived, *wd, scales), page_slots.reshape(1, -1))

    def shift(v, by):
        return lax.ppermute(v, "y", [(i, (i + by) % n_y) for i in range(n_y)])

    with jax.named_scope("rows"):
        p_left, p_right = shift(x_p, 1), shift(x_p, -1)
        p_far = shift(p_left, 1)
        q_right = shift(after(x_q, p_right, p_left), -1)
        q_left = shift(after(x_q, p_far), 1)
        q_far = shift(q_right, -1)

    with jax.named_scope("swap"):
        w2 = [lax.ppermute(w, "core", swap) for w in (other_g, other_u)]

    units = n_core * hid

    def columns(k, p, steps):
        by = steps[0]
        for i, s in enumerate(steps[1:], 1):
            by = jnp.where(k == i, s, by)
        return lax.rem(p[0] + by, n_y)

    def weight_specs(*steps):
        def own():
            return pl.BlockSpec((1, hid, quarter), lambda k, p: (p[1], 0, columns(k, p, steps)))

        def other():
            return pl.BlockSpec((1, hid, quarter), lambda k, p: (0, 0, columns(k, p, steps)))

        return [own(), other(), own(), other()]

    def call(kernel, steps, in_specs, out_specs, out_shape, scratch=(), params=PARAMS):
        return pl.pallas_call(
            kernel,
            grid_spec=pltpu.PrefetchScalarGridSpec(
                num_scalar_prefetch=1,
                grid=(steps,),
                in_specs=in_specs,
                out_specs=out_specs,
                scratch_shapes=list(scratch),
            ),
            out_shape=out_shape,
            compiler_params=params,
            cost_estimate=CHEAP,
        )

    weights = (w_gate, w2[0], w_up, w2[1])
    channel = pl.BlockSpec((1, 1, quarter), lambda k, p: (p[1], 0, p[0]))
    down_scale = down_scale.reshape(experts, 1, width)

    def acc(r):
        return [pltpu.VMEM((r, 2 * units), F32)]

    with jax.named_scope("up"):
        r = rows
        both_p = call(
            up_first_kernel,
            3,
            [whole(r, quarter)] * 3 + weight_specs(0, 3, 1),
            whole(r, 2 * units),
            sds(r, 2 * units, dtype=F32),
        )(place, x_p, p_left, p_right, *weights)
        h_p = call(
            up_last_kernel,
            1,
            [whole(r, quarter)] + weight_specs(2) + [whole(r, 2 * units), whole(2, units)],
            whole(r, units),
            sds(r, units),
            acc(r),
        )(place, p_far, *weights, both_p, scales)

    with jax.named_scope("up"):
        r = rows + rows // 2
        both_q = call(
            up_first_kernel,
            2,
            [whole(r, quarter)] * 2 + weight_specs(0, 1),
            whole(r, 2 * units),
            sds(r, 2 * units, dtype=F32),
        )(place, x_q, q_right, *weights)
    with jax.named_scope("down"):
        near = [shift(h_p, 1), shift(h_p, -1), shift(h_p, 2)]
        near[2] = after(near[2], both_q)
        r = rows
        v_p = call(
            down_kernel,
            1,
            [whole(r, units)] * 4 + [whole(hid, quarter)] * 8 + [channel],
            whole(r, quarter),
            sds(r, quarter),
            params=SMALL,
        )(place, h_p, *near, *wd, down_scale)
        back_p = exchange(v_p)

    with jax.named_scope("up"):
        r = rows + rows // 2
        h_q = call(
            up_last_kernel,
            2,
            [whole(r, quarter)] * 2 + weight_specs(3, 2) + [whole(r, 2 * units), whole(2, units)],
            whole(r, units),
            sds(r, units),
            acc(r),
        )(place, q_left, q_far, *weights, both_q, scales)

    with jax.named_scope("down"):
        near = [shift(h_q, 1), shift(h_q, -1), shift(h_q, 2)]
        part = pl.pallas_call(
            down_first_kernel,
            out_shape=sds(r, quarter, dtype=F32),
            compiler_params=SMALL,
            cost_estimate=CHEAP,
        )(h_q, *wd[:2])
        v_q = call(
            down_last_kernel,
            1,
            [whole(r, units)] * 3
            + [whole(hid, quarter)] * 6
            + [whole(r, quarter), channel, whole(rows, kv_cols)],
            whole(rows, payload),
            sds(rows, payload),
            params=SMALL,
        )(place, *near, *wd[2:], part, down_scale, kv_q)
        back_q = exchange(v_q)

    with jax.named_scope("combine"):
        total, picked = pl.pallas_call(
            functools.partial(combine_first_kernel, n_dp),
            in_specs=[smem] + [vmem] * 3,
            out_shape=[sds(tok, quarter, dtype=F32), sds(6, rows, tok)],
            compiler_params=SMALL,
            cost_estimate=CHEAP,
        )(place, ids_t, gates_t, back_p)
        keep, send, kv_cache = pl.pallas_call(
            combine_last_kernel,
            in_specs=[smem] + [vmem] * 3,
            out_shape=[sds(tok, half, dtype=F32), sds(tok, half, dtype=F32), sds(tok, kv_cols)],
            compiler_params=SMALL,
            cost_estimate=CHEAP,
        )(place, picked, total, back_q)
        moe_out = (keep + lax.ppermute(send, "core", [(0, 1), (1, 0)])).astype(BF)
    return moe_out, kv_cache.reshape(tok // PAGE, PAGE, kv_cols)


def solution(mesh):
    shape = mesh.devices.shape
    n_z, n_x, n_y = 8, 4, 4
    fine = Mesh(np.asarray(mesh.devices).reshape(n_z, n_x, n_y, shape[1] // n_y), ("z", "x", "y", "core"))
    group = ("y", "core")
    placed = (
        P(DP, None),
        P(DP, None),
        P(DP, None),
        P(DP, group, None),
        P(DP, group, None),
        P(DP, group, None),
        P(DP, group),
        P(DP, group),
        P(DP, None),
        P(DP, group),
        P(),
    )
    return jax.shard_map(
        on_device,
        mesh=fine,
        in_specs=placed,
        out_specs=(P(DP, group), P(DP, None, group)),
        check_vma=False,
    )
```

```python
import functools

import jax
import jax.numpy as jnp
import numpy as np
from jax import lax
from jax.experimental import pallas as pl
from jax.experimental.pallas import tpu as pltpu
from jax.sharding import Mesh
from jax.sharding import PartitionSpec as P

BF = jnp.bfloat16
F32 = jnp.float32
PAGE = 32
ROWS = 8
DP = ("z", "x")
MOVES = ((0, False), (0, True), (1, False), (1, True), (3, False), (3, True), (2, False), (2, True))


def dot(a, b):
    return lax.dot_general(a, b, (((1,), (0,)), ((), ())), preferred_element_type=F32)


def dot_nt(a, b):
    return lax.dot_general(a, b, (((1,), (1,)), ((), ())), preferred_element_type=F32)


def dot_tn(a, b):
    return lax.dot_general(a, b, (((0,), (0,)), ((), ())), preferred_element_type=F32)


def iota(shape, dim):
    return lax.broadcasted_iota(jnp.int32, shape, dim)


def ones(cond, dtype=BF):
    return jnp.where(cond, 1.0, 0.0).astype(dtype)


def slot_codes(ids_t, parity, n_dst, none):
    picks, tok = ids_t.shape
    expert = 2 * iota((n_dst, tok), 0) + parity
    named = jnp.zeros((n_dst, tok), F32)
    for k in range(picks):
        named = named + ones(ids_t[k : k + 1, :] == expert, F32)
    earlier = ones(iota((tok, tok), 0) < iota((tok, tok), 1))
    place = dot(named.astype(BF), earlier)
    code = jnp.where(named > 0, place, none)
    spread = ones((iota((n_dst * ROWS, n_dst), 0) // ROWS) == iota((n_dst * ROWS, n_dst), 1))
    return dot(spread, code.astype(BF)), spread


def selections(code):
    row = iota(code.shape, 0) % ROWS
    slot = row.astype(F32)
    low = row < 4
    return (
        code == slot,
        code == slot + 8.0,
        (code == slot + 16.0) & low,
        (code == slot + 12.0) & jnp.logical_not(low),
    )


def route_kernel(n_dst, place_ref, ids_ref, tok_hbm, kv_ref, wd_hbm, out_ref, *refs):
    cuts, (tok_ref, sems) = refs[:-2], refs[-2:]
    quarter = tok_ref.shape[1]
    half = quarter // 2
    y, core = place_ref[0], place_ref[1]
    cols = pl.ds(pl.multiple_of(y * quarter, quarter), quarter)
    copies = [(tok_hbm.at[:, cols], tok_ref)]
    for (by, other), cut in zip(MOVES, cuts):
        cols = pl.ds(pl.multiple_of(lax.rem(y + by, 4) * quarter, quarter), quarter)
        copies.append((wd_hbm.at[1 - core if other else core, :, cols], cut))
    copies = [pltpu.make_async_copy(a, b, sems.at[i]) for i, (a, b) in enumerate(copies)]
    for c in copies:
        c.start()
    code, _ = slot_codes(ids_ref[...], place_ref[1], n_dst, 200.0)
    first, second, low, high = selections(code)
    n, t = code.shape
    row, col = iota((n, t), 0), iota((n, t), 1)
    piece = (col == (row % ROWS) * PAGE + row // ROWS) & (row % ROWS < t // PAGE)
    out_ref[:, 2 * quarter + half :] = dot(ones(piece), kv_ref[...]).astype(BF)
    copies[0].wait()
    tok = tok_ref[...]
    out_ref[:, :quarter] = dot(ones(first), tok).astype(BF)
    out_ref[:, quarter : 2 * quarter] = dot(ones(second), tok).astype(BF)
    out_ref[:, 2 * quarter : 2 * quarter + half] = (
        dot(ones(low), tok[:, :half]) + dot(ones(high), tok[:, half:])
    ).astype(BF)
    for c in copies[1:]:
        c.wait()


def other_kernel(place_ref, wg_ref, wu_ref, g_ref, u_ref, sems):
    sibling = pl.ds(1 - place_ref[1], 1)
    copies = [(wg_ref.at[sibling], g_ref), (wu_ref.at[sibling], u_ref)]
    copies = [pltpu.make_async_copy(a, b, sems.at[i]) for i, (a, b) in enumerate(copies)]
    for c in copies:
        c.start()
    for c in copies:
        c.wait()


def unpack_kernel(in_ref, slots_ref, p_ref, q_ref, kv_ref):
    n = in_ref.shape[0]
    quarter = q_ref.shape[1]
    half = quarter // 2
    p_ref[...] = in_ref[:, :quarter]
    q_ref[:n] = in_ref[:, quarter : 2 * quarter]
    m = n // 2
    row, col = iota((m, n), 0), iota((m, n), 1)
    at = (row // 4) * ROWS + row % 4
    mixed = in_ref[:, 2 * quarter : 2 * quarter + half]
    q_ref[n:, :half] = dot(ones(col == at), mixed).astype(BF)
    q_ref[n:, half:] = dot(ones(col == at + 4), mixed).astype(BF)
    pages = slots_ref.shape[1]
    row, col = iota((pages, n), 0), iota((pages, n), 1)
    held = col % ROWS < 4
    spread = ones(held & (row == (col // ROWS) * 4 + col % ROWS))
    slots = jnp.broadcast_to(slots_ref[...].astype(F32), (8, pages)).astype(BF)
    slots = jnp.where(held[0:1], dot(slots, spread)[0:1], -2.0)
    row = iota((n, n), 0)
    wanted = jnp.where(row % ROWS < 4, (row // ROWS) * 4 + row % ROWS, -1).astype(F32)
    kv_ref[...] = dot(ones(slots == wanted), in_ref[:, 2 * quarter + half :]).astype(BF)


def gated(both, s_ref):
    n = s_ref.shape[1]
    g, u = both[:, :n] * s_ref[0:1, :], both[:, n:] * s_ref[1:2, :]
    return (g / (1.0 + jnp.exp(-g)) * u).astype(BF)


def up_step(acc_ref, x_ref, w_refs, first):
    w = jnp.concatenate([ref[0] for ref in w_refs], axis=0)
    both = dot_nt(x_ref[...], w)
    if first:
        acc_ref[...] = both
    else:
        acc_ref[...] += both


def up_first_kernel(place_ref, *refs):
    *x_refs, w0, w1, w2, w3, acc_ref = refs
    k = pl.program_id(0)
    for i, x_ref in enumerate(x_refs):
        pl.when(k == i)(functools.partial(up_step, acc_ref, x_ref, (w0, w1, w2, w3), i == 0))


def up_last_kernel(place_ref, *refs):
    *x_refs, w0, w1, w2, w3, part_ref, s_ref, out_ref, acc_ref = refs
    k = pl.program_id(0)
    for i, x_ref in enumerate(x_refs):
        pl.when(k == i)(functools.partial(up_step, acc_ref, x_ref, (w0, w1, w2, w3), i == 0))

    @pl.when(k == len(x_refs) - 1)
    def _():
        out_ref[...] = gated(acc_ref[...] + part_ref[...], s_ref)


def down_sum(h_refs, w_refs):
    acc = None
    for i, h_ref in enumerate(h_refs):
        w = jnp.concatenate([w_refs[2 * i][...], w_refs[2 * i + 1][...]], axis=0)
        part = dot(h_ref[...], w)
        acc = part if acc is None else acc + part
    return acc


def down_kernel(place_ref, *refs):
    refs[13][...] = (down_sum(refs[:4], refs[4:12]) * refs[12][0]).astype(BF)


def down_first_kernel(h_ref, same_ref, cross_ref, out_ref):
    out_ref[...] = down_sum((h_ref,), (same_ref, cross_ref))


def down_last_kernel(place_ref, *refs):
    acc_ref, s_ref, kv_ref, out_ref = refs[9:]
    y = ((acc_ref[...] + down_sum(refs[:3], refs[3:9])) * s_ref[0]).astype(BF)
    n, quarter = kv_ref.shape[0], y.shape[1]
    half = quarter // 2
    out_ref[:, :quarter] = y[:n]
    rest = y[n:]
    m = n // 2
    row, col = iota((n, m), 0), iota((n, m), 1)
    hit = col == (row // ROWS) * 4 + row % 4
    low = row % ROWS < 4
    out_ref[:, quarter : quarter + half] = (
        dot(ones(hit & low), rest[:, :half]) + dot(ones(hit & jnp.logical_not(low)), rest[:, half:])
    ).astype(BF)
    out_ref[:, quarter + half :] = kv_ref[...]


def combine_first_kernel(n_dst, place_ref, ids_ref, gates_ref, in_ref, acc_ref, gates_out_ref):
    parity = place_ref[1]
    ids, gates = ids_ref[...], gates_ref[...]
    code, spread = slot_codes(ids, parity, n_dst, 200.0)
    picks, tok = ids.shape
    expert = 2 * iota((n_dst, tok), 0) + parity
    gate = jnp.zeros((n_dst, tok), F32)
    for k in range(picks):
        gate = gate + jnp.where(ids[k : k + 1, :] == expert, gates[k : k + 1, :], 0.0)
    top = gate.astype(BF)
    rest = (gate - top.astype(F32)).astype(BF)
    top, rest = dot(spread, top), dot(spread, rest)
    first, *others = selections(code)
    for i, where in enumerate(others):
        gates_out_ref[2 * i] = jnp.where(where, top, 0.0).astype(BF)
        gates_out_ref[2 * i + 1] = jnp.where(where, rest, 0.0).astype(BF)
    acc_ref[...] = dot_tn(jnp.where(first, top, 0.0).astype(BF), in_ref[...]) + dot_tn(
        jnp.where(first, rest, 0.0).astype(BF), in_ref[...]
    )


def combine_last_kernel(place_ref, g_ref, acc_ref, in_ref, keep_ref, send_ref, kv_ref):
    half = keep_ref.shape[1]
    quarter = 2 * half
    rows = in_ref[:, :quarter]
    mixed = in_ref[:, quarter : quarter + half]
    sums = acc_ref[...] + dot_tn(g_ref[0], rows) + dot_tn(g_ref[1], rows)
    low = sums[:, :half] + dot_tn(g_ref[2], mixed) + dot_tn(g_ref[3], mixed)
    high = sums[:, half:] + dot_tn(g_ref[4], mixed) + dot_tn(g_ref[5], mixed)
    even = place_ref[1] == 0
    keep_ref[...] = jnp.where(even, low, high)
    send_ref[...] = jnp.where(even, high, low)
    n, tok = in_ref.shape[0], keep_ref.shape[0]
    row, col = iota((tok, n), 0), iota((tok, n), 1)
    kv_ref[...] = dot(ones(col == (row % PAGE) * ROWS + row // PAGE), in_ref[:, quarter + half :]).astype(BF)


def sds(*shape, dtype=BF):
    return jax.ShapeDtypeStruct(shape, dtype)


def whole(*shape):
    return pl.BlockSpec(shape, lambda *a: (0,) * len(shape))


CHEAP = pl.CostEstimate(flops=1000, bytes_accessed=1000, transcendentals=0)
PARAMS = pltpu.CompilerParams(vmem_limit_bytes=62 * 1024 * 1024)
SMALL = pltpu.CompilerParams(vmem_limit_bytes=24 * 1024 * 1024)


def on_device(
    tokens, expert_ids, gates, w_gate, w_up, w_down, gate_scale, up_scale, down_scale, kv_rows, page_slots
):
    y, core = lax.axis_index("y"), lax.axis_index("core")
    n_dp = lax.axis_size("z") * lax.axis_size("x")
    n_y, n_core = lax.axis_size("y"), lax.axis_size("core")
    tok, width = tokens.shape
    quarter = width // n_y
    half = quarter // 2
    experts, hid = w_gate.shape[:2]
    kv_cols = kv_rows.shape[1]
    rows = n_dp * ROWS
    place = jnp.stack([y, core]).astype(jnp.int32)
    ids_t, gates_t = expert_ids.T, gates.T
    picks = ids_t.shape[0]

    payload = quarter + half + kv_cols
    hbm = pl.BlockSpec(memory_space=pltpu.HBM)
    vmem = pl.BlockSpec(memory_space=pltpu.VMEM)
    smem = pl.BlockSpec(memory_space=pltpu.SMEM)
    swap = [(0, 1), (1, 0)]

    def after(v, *others):
        return lax.optimization_barrier((v, *others))[0]

    with jax.named_scope("route"):
        outgoing, *cuts = pl.pallas_call(
            functools.partial(route_kernel, n_dp),
            in_specs=[smem, vmem, hbm, vmem, hbm],
            out_specs=[vmem] * 9,
            out_shape=[sds(rows, quarter + payload)] + [sds(hid, quarter)] * 8,
            scratch_shapes=[pltpu.VMEM((tok, quarter), BF), pltpu.SemaphoreType.DMA((9,))],
            compiler_params=PARAMS,
            cost_estimate=CHEAP,
        )(place, ids_t, tokens, kv_rows, w_down)
        other_g, other_u = pl.pallas_call(
            other_kernel,
            in_specs=[smem, hbm, hbm],
            out_specs=[vmem] * 2,
            out_shape=[sds(1, hid, width)] * 2,
            scratch_shapes=[pltpu.SemaphoreType.DMA((2,))],
            compiler_params=PARAMS,
            cost_estimate=CHEAP,
        )(place, after(w_gate, outgoing), w_up)
        wd = [cuts[0]]
        for (by, other), v in zip(MOVES[1:], cuts[1:]):
            pairs = [
                (i * n_core + c, (i + by) % n_y * n_core + (1 - c if other else c))
                for i in range(n_y)
                for c in range(n_core)
            ]
            if len(wd) == 7:
                v = after(v, other_g)
            wd.append(lax.ppermute(v, ("y", "core"), pairs))

    def exchange(v):
        return lax.all_to_all(v.reshape(n_dp, ROWS, v.shape[-1]), DP, 0, 0, tiled=True).reshape(v.shape)

    with jax.named_scope("dispatch"):
        arrived = exchange(outgoing)

    with jax.named_scope("scales"):
        both = jnp.stack([gate_scale, up_scale])
        own = lax.dynamic_index_in_dim(both, core, 1, keepdims=False)
        other = lax.ppermute(lax.dynamic_index_in_dim(both, 1 - core, 1, keepdims=False), "core", swap)
        scales = jnp.concatenate([own, other], axis=1)

    with jax.named_scope("unpack"):
        x_p, x_q, kv_q = pl.pallas_call(
            unpack_kernel,
            out_shape=[sds(rows, quarter), sds(rows + rows // 2, quarter), sds(rows, kv_cols)],
            compiler_params=PARAMS,
            cost_estimate=CHEAP,
        )(after(arrived, *wd, scales), page_slots.reshape(1, -1))

    def shift(v, by):
        return lax.ppermute(v, "y", [(i, (i + by) % n_y) for i in range(n_y)])

    with jax.named_scope("rows"):
        p_left, p_right = shift(x_p, 1), shift(x_p, -1)
        p_far = shift(p_left, 1)
        q_right = shift(after(x_q, p_right, p_left), -1)
        q_left = shift(after(x_q, p_far), 1)
        q_far = shift(q_right, -1)

    with jax.named_scope("swap"):
        w2 = [lax.ppermute(w, "core", swap) for w in (other_g, other_u)]

    units = n_core * hid

    def columns(k, p, steps):
        by = steps[0]
        for i, s in enumerate(steps[1:], 1):
            by = jnp.where(k == i, s, by)
        return lax.rem(p[0] + by, n_y)

    def weight_specs(*steps):
        def own():
            return pl.BlockSpec((1, hid, quarter), lambda k, p: (p[1], 0, columns(k, p, steps)))

        def other():
            return pl.BlockSpec((1, hid, quarter), lambda k, p: (0, 0, columns(k, p, steps)))

        return [own(), other(), own(), other()]

    def call(kernel, steps, in_specs, out_specs, out_shape, scratch=(), params=PARAMS):
        return pl.pallas_call(
            kernel,
            grid_spec=pltpu.PrefetchScalarGridSpec(
                num_scalar_prefetch=1,
                grid=(steps,),
                in_specs=in_specs,
                out_specs=out_specs,
                scratch_shapes=list(scratch),
            ),
            out_shape=out_shape,
            compiler_params=params,
            cost_estimate=CHEAP,
        )

    weights = (w_gate, w2[0], w_up, w2[1])
    channel = pl.BlockSpec((1, 1, quarter), lambda k, p: (p[1], 0, p[0]))
    down_scale = down_scale.reshape(experts, 1, width)

    def acc(r):
        return [pltpu.VMEM((r, 2 * units), F32)]

    with jax.named_scope("up"):
        r = rows
        both_p = call(
            up_first_kernel,
            3,
            [whole(r, quarter)] * 3 + weight_specs(0, 3, 1),
            whole(r, 2 * units),
            sds(r, 2 * units, dtype=F32),
        )(place, x_p, p_left, p_right, *weights)
        h_p = call(
            up_last_kernel,
            1,
            [whole(r, quarter)] + weight_specs(2) + [whole(r, 2 * units), whole(2, units)],
            whole(r, units),
            sds(r, units),
            acc(r),
        )(place, p_far, *weights, both_p, scales)

    with jax.named_scope("up"):
        r = rows + rows // 2
        both_q = call(
            up_first_kernel,
            2,
            [whole(r, quarter)] * 2 + weight_specs(0, 1),
            whole(r, 2 * units),
            sds(r, 2 * units, dtype=F32),
        )(place, x_q, q_right, *weights)
    with jax.named_scope("down"):
        near = [shift(h_p, 1), shift(h_p, -1), shift(h_p, 2)]
        near[2] = after(near[2], both_q)
        r = rows
        v_p = call(
            down_kernel,
            1,
            [whole(r, units)] * 4 + [whole(hid, quarter)] * 8 + [channel],
            whole(r, quarter),
            sds(r, quarter),
        )(place, h_p, *near, *wd, down_scale)
        back_p = exchange(v_p)

    with jax.named_scope("up"):
        r = rows + rows // 2
        h_q = call(
            up_last_kernel,
            2,
            [whole(r, quarter)] * 2 + weight_specs(3, 2) + [whole(r, 2 * units), whole(2, units)],
            whole(r, units),
            sds(r, units),
            acc(r),
        )(place, q_left, q_far, *weights, both_q, scales)

    with jax.named_scope("down"):
        near = [shift(h_q, 1), shift(h_q, -1), shift(h_q, 2)]
        part = pl.pallas_call(
            down_first_kernel,
            out_shape=sds(r, quarter, dtype=F32),
            compiler_params=SMALL,
            cost_estimate=CHEAP,
        )(h_q, *wd[:2])
        v_q = call(
            down_last_kernel,
            1,
            [whole(r, units)] * 3
            + [whole(hid, quarter)] * 6
            + [whole(r, quarter), channel, whole(rows, kv_cols)],
            whole(rows, payload),
            sds(rows, payload),
            params=SMALL,
        )(place, *near, *wd[2:], part, down_scale, kv_q)
        back_q = exchange(v_q)

    with jax.named_scope("combine"):
        total, picked = pl.pallas_call(
            functools.partial(combine_first_kernel, n_dp),
            in_specs=[smem] + [vmem] * 3,
            out_shape=[sds(tok, quarter, dtype=F32), sds(6, rows, tok)],
            compiler_params=SMALL,
            cost_estimate=CHEAP,
        )(place, ids_t, gates_t, back_p)
        keep, send, kv_cache = pl.pallas_call(
            combine_last_kernel,
            in_specs=[smem] + [vmem] * 3,
            out_shape=[sds(tok, half, dtype=F32), sds(tok, half, dtype=F32), sds(tok, kv_cols)],
            compiler_params=SMALL,
            cost_estimate=CHEAP,
        )(place, picked, total, back_q)
        moe_out = (keep + lax.ppermute(send, "core", [(0, 1), (1, 0)])).astype(BF)
    return moe_out, kv_cache.reshape(tok // PAGE, PAGE, kv_cols)


def solution(mesh):
    shape = mesh.devices.shape
    n_z, n_x, n_y = 8, 4, 4
    fine = Mesh(np.asarray(mesh.devices).reshape(n_z, n_x, n_y, shape[1] // n_y), ("z", "x", "y", "core"))
    group = ("y", "core")
    placed = (
        P(DP, None),
        P(DP, None),
        P(DP, None),
        P(DP, group, None),
        P(DP, group, None),
        P(DP, group, None),
        P(DP, group),
        P(DP, group),
        P(DP, None),
        P(DP, group),
        P(),
    )
    return jax.shard_map(
        on_device,
        mesh=fine,
        in_specs=placed,
        out_specs=(P(DP, group), P(DP, None, group)),
        check_vma=False,
    )
```

```python
import functools

import jax
import jax.numpy as jnp
import numpy as np
from jax import lax
from jax.experimental import pallas as pl
from jax.experimental.pallas import tpu as pltpu
from jax.sharding import Mesh
from jax.sharding import PartitionSpec as P

BF = jnp.bfloat16
F32 = jnp.float32
PAGE = 32
ROWS = 8
DP = ("z", "x")
MOVES = ((0, False), (0, True), (1, False), (1, True), (3, False), (3, True), (2, False), (2, True))


def dot(a, b):
    return lax.dot_general(a, b, (((1,), (0,)), ((), ())), preferred_element_type=F32)


def dot_nt(a, b):
    return lax.dot_general(a, b, (((1,), (1,)), ((), ())), preferred_element_type=F32)


def dot_tn(a, b):
    return lax.dot_general(a, b, (((0,), (0,)), ((), ())), preferred_element_type=F32)


def iota(shape, dim):
    return lax.broadcasted_iota(jnp.int32, shape, dim)


def ones(cond, dtype=BF):
    return jnp.where(cond, 1.0, 0.0).astype(dtype)


def slot_codes(ids_t, parity, n_dst, none):
    picks, tok = ids_t.shape
    expert = 2 * iota((n_dst, tok), 0) + parity
    named = jnp.zeros((n_dst, tok), F32)
    for k in range(picks):
        named = named + ones(ids_t[k : k + 1, :] == expert, F32)
    earlier = ones(iota((tok, tok), 0) < iota((tok, tok), 1))
    place = dot(named.astype(BF), earlier)
    code = jnp.where(named > 0, place, none)
    spread = ones((iota((n_dst * ROWS, n_dst), 0) // ROWS) == iota((n_dst * ROWS, n_dst), 1))
    return dot(spread, code.astype(BF)), spread


def selections(code):
    row = iota(code.shape, 0) % ROWS
    slot = row.astype(F32)
    low = row < 4
    return (
        code == slot,
        code == slot + 8.0,
        (code == slot + 16.0) & low,
        (code == slot + 12.0) & jnp.logical_not(low),
    )


def route_kernel(n_dst, place_ref, ids_ref, tok_hbm, kv_ref, wd_hbm, out_ref, *refs):
    cuts, (tok_ref, sems) = refs[:-2], refs[-2:]
    quarter = tok_ref.shape[1]
    half = quarter // 2
    y, core = place_ref[0], place_ref[1]
    cols = pl.ds(pl.multiple_of(y * quarter, quarter), quarter)
    copies = [(tok_hbm.at[:, cols], tok_ref)]
    for (by, other), cut in zip(MOVES, cuts):
        cols = pl.ds(pl.multiple_of(lax.rem(y + by, 4) * quarter, quarter), quarter)
        copies.append((wd_hbm.at[1 - core if other else core, :, cols], cut))
    copies = [pltpu.make_async_copy(a, b, sems.at[i]) for i, (a, b) in enumerate(copies)]
    for c in copies:
        c.start()
    code, _ = slot_codes(ids_ref[...], place_ref[1], n_dst, 200.0)
    first, second, low, high = selections(code)
    n, t = code.shape
    row, col = iota((n, t), 0), iota((n, t), 1)
    piece = (col == (row % ROWS) * PAGE + row // ROWS) & (row % ROWS < t // PAGE)
    out_ref[:, 2 * quarter + half :] = dot(ones(piece), kv_ref[...]).astype(BF)
    copies[0].wait()
    tok = tok_ref[...]
    out_ref[:, :quarter] = dot(ones(first), tok).astype(BF)
    out_ref[:, quarter : 2 * quarter] = dot(ones(second), tok).astype(BF)
    out_ref[:, 2 * quarter : 2 * quarter + half] = (
        dot(ones(low), tok[:, :half]) + dot(ones(high), tok[:, half:])
    ).astype(BF)
    for c in copies[1:]:
        c.wait()


def other_kernel(place_ref, wg_ref, wu_ref, g_ref, u_ref, sems):
    sibling = pl.ds(1 - place_ref[1], 1)
    copies = [(wg_ref.at[sibling], g_ref), (wu_ref.at[sibling], u_ref)]
    copies = [pltpu.make_async_copy(a, b, sems.at[i]) for i, (a, b) in enumerate(copies)]
    for c in copies:
        c.start()
    for c in copies:
        c.wait()


def unpack_kernel(in_ref, slots_ref, p_ref, q_ref, kv_ref):
    n = in_ref.shape[0]
    quarter = q_ref.shape[1]
    half = quarter // 2
    p_ref[...] = in_ref[:, :quarter]
    q_ref[:n] = in_ref[:, quarter : 2 * quarter]
    m = n // 2
    row, col = iota((m, n), 0), iota((m, n), 1)
    at = (row // 4) * ROWS + row % 4
    mixed = in_ref[:, 2 * quarter : 2 * quarter + half]
    q_ref[n:, :half] = dot(ones(col == at), mixed).astype(BF)
    q_ref[n:, half:] = dot(ones(col == at + 4), mixed).astype(BF)
    pages = slots_ref.shape[1]
    row, col = iota((pages, n), 0), iota((pages, n), 1)
    held = col % ROWS < 4
    spread = ones(held & (row == (col // ROWS) * 4 + col % ROWS))
    slots = jnp.broadcast_to(slots_ref[...].astype(F32), (8, pages)).astype(BF)
    slots = jnp.where(held[0:1], dot(slots, spread)[0:1], -2.0)
    row = iota((n, n), 0)
    wanted = jnp.where(row % ROWS < 4, (row // ROWS) * 4 + row % ROWS, -1).astype(F32)
    kv_ref[...] = dot(ones(slots == wanted), in_ref[:, 2 * quarter + half :]).astype(BF)


def gated(both, s_ref):
    n = s_ref.shape[1]
    g, u = both[:, :n] * s_ref[0:1, :], both[:, n:] * s_ref[1:2, :]
    return (g / (1.0 + jnp.exp(-g)) * u).astype(BF)


def up_step(acc_ref, x_ref, w_refs, first):
    w = jnp.concatenate([ref[0] for ref in w_refs], axis=0)
    both = dot_nt(x_ref[...], w)
    if first:
        acc_ref[...] = both
    else:
        acc_ref[...] += both


def up_first_kernel(place_ref, *refs):
    *x_refs, w0, w1, w2, w3, acc_ref = refs
    k = pl.program_id(0)
    for i, x_ref in enumerate(x_refs):
        pl.when(k == i)(functools.partial(up_step, acc_ref, x_ref, (w0, w1, w2, w3), i == 0))


def up_last_kernel(place_ref, *refs):
    *x_refs, w0, w1, w2, w3, part_ref, s_ref, out_ref, acc_ref = refs
    k = pl.program_id(0)
    for i, x_ref in enumerate(x_refs):
        pl.when(k == i)(functools.partial(up_step, acc_ref, x_ref, (w0, w1, w2, w3), i == 0))

    @pl.when(k == len(x_refs) - 1)
    def _():
        out_ref[...] = gated(acc_ref[...] + part_ref[...], s_ref)


def down_sum(h_refs, w_refs):
    acc = None
    for i, h_ref in enumerate(h_refs):
        w = jnp.concatenate([w_refs[2 * i][...], w_refs[2 * i + 1][...]], axis=0)
        part = dot(h_ref[...], w)
        acc = part if acc is None else acc + part
    return acc


def down_kernel(place_ref, *refs):
    refs[13][...] = (down_sum(refs[:4], refs[4:12]) * refs[12][0]).astype(BF)


def down_first_kernel(h_ref, same_ref, cross_ref, out_ref):
    out_ref[...] = down_sum((h_ref,), (same_ref, cross_ref))


def down_last_kernel(place_ref, *refs):
    acc_ref, s_ref, kv_ref, out_ref = refs[9:]
    y = ((acc_ref[...] + down_sum(refs[:3], refs[3:9])) * s_ref[0]).astype(BF)
    n, quarter = kv_ref.shape[0], y.shape[1]
    half = quarter // 2
    out_ref[:, :quarter] = y[:n]
    rest = y[n:]
    m = n // 2
    row, col = iota((n, m), 0), iota((n, m), 1)
    hit = col == (row // ROWS) * 4 + row % 4
    low = row % ROWS < 4
    out_ref[:, quarter : quarter + half] = (
        dot(ones(hit & low), rest[:, :half]) + dot(ones(hit & jnp.logical_not(low)), rest[:, half:])
    ).astype(BF)
    out_ref[:, quarter + half :] = kv_ref[...]


def combine_first_kernel(n_dst, place_ref, ids_ref, gates_ref, in_ref, acc_ref, gates_out_ref):
    parity = place_ref[1]
    ids, gates = ids_ref[...], gates_ref[...]
    code, spread = slot_codes(ids, parity, n_dst, 200.0)
    picks, tok = ids.shape
    expert = 2 * iota((n_dst, tok), 0) + parity
    gate = jnp.zeros((n_dst, tok), F32)
    for k in range(picks):
        gate = gate + jnp.where(ids[k : k + 1, :] == expert, gates[k : k + 1, :], 0.0)
    top = gate.astype(BF)
    rest = (gate - top.astype(F32)).astype(BF)
    top, rest = dot(spread, top), dot(spread, rest)
    first, *others = selections(code)
    for i, where in enumerate(others):
        gates_out_ref[2 * i] = jnp.where(where, top, 0.0).astype(BF)
        gates_out_ref[2 * i + 1] = jnp.where(where, rest, 0.0).astype(BF)
    acc_ref[...] = dot_tn(jnp.where(first, top, 0.0).astype(BF), in_ref[...]) + dot_tn(
        jnp.where(first, rest, 0.0).astype(BF), in_ref[...]
    )


def combine_last_kernel(place_ref, g_ref, acc_ref, in_ref, keep_ref, send_ref, kv_ref):
    half = keep_ref.shape[1]
    quarter = 2 * half
    rows = in_ref[:, :quarter]
    mixed = in_ref[:, quarter : quarter + half]
    sums = acc_ref[...] + dot_tn(g_ref[0], rows) + dot_tn(g_ref[1], rows)
    low = sums[:, :half] + dot_tn(g_ref[2], mixed) + dot_tn(g_ref[3], mixed)
    high = sums[:, half:] + dot_tn(g_ref[4], mixed) + dot_tn(g_ref[5], mixed)
    even = place_ref[1] == 0
    keep_ref[...] = jnp.where(even, low, high)
    send_ref[...] = jnp.where(even, high, low)
    n, tok = in_ref.shape[0], keep_ref.shape[0]
    row, col = iota((tok, n), 0), iota((tok, n), 1)
    kv_ref[...] = dot(ones(col == (row % PAGE) * ROWS + row // PAGE), in_ref[:, quarter + half :]).astype(BF)


def sds(*shape, dtype=BF):
    return jax.ShapeDtypeStruct(shape, dtype)


def whole(*shape):
    return pl.BlockSpec(shape, lambda *a: (0,) * len(shape))


CHEAP = pl.CostEstimate(flops=1000, bytes_accessed=1000, transcendentals=0)
PARAMS = pltpu.CompilerParams(vmem_limit_bytes=62 * 1024 * 1024)
SMALL = pltpu.CompilerParams(vmem_limit_bytes=24 * 1024 * 1024)


def on_device(
    tokens, expert_ids, gates, w_gate, w_up, w_down, gate_scale, up_scale, down_scale, kv_rows, page_slots
):
    y, core = lax.axis_index("y"), lax.axis_index("core")
    n_dp = lax.axis_size("z") * lax.axis_size("x")
    n_y, n_core = lax.axis_size("y"), lax.axis_size("core")
    tok, width = tokens.shape
    quarter = width // n_y
    half = quarter // 2
    experts, hid = w_gate.shape[:2]
    kv_cols = kv_rows.shape[1]
    rows = n_dp * ROWS
    place = jnp.stack([y, core]).astype(jnp.int32)
    ids_t, gates_t = expert_ids.T, gates.T
    picks = ids_t.shape[0]

    payload = quarter + half + kv_cols
    hbm = pl.BlockSpec(memory_space=pltpu.HBM)
    vmem = pl.BlockSpec(memory_space=pltpu.VMEM)
    smem = pl.BlockSpec(memory_space=pltpu.SMEM)
    swap = [(0, 1), (1, 0)]

    def after(v, *others):
        return lax.optimization_barrier((v, *others))[0]

    with jax.named_scope("route"):
        outgoing, *cuts = pl.pallas_call(
            functools.partial(route_kernel, n_dp),
            in_specs=[smem, vmem, hbm, vmem, hbm],
            out_specs=[vmem] * 9,
            out_shape=[sds(rows, quarter + payload)] + [sds(hid, quarter)] * 8,
            scratch_shapes=[pltpu.VMEM((tok, quarter), BF), pltpu.SemaphoreType.DMA((9,))],
            compiler_params=PARAMS,
            cost_estimate=CHEAP,
        )(place, ids_t, tokens, kv_rows, w_down)
        other_g, other_u = pl.pallas_call(
            other_kernel,
            in_specs=[smem, hbm, hbm],
            out_specs=[vmem] * 2,
            out_shape=[sds(1, hid, width)] * 2,
            scratch_shapes=[pltpu.SemaphoreType.DMA((2,))],
            compiler_params=PARAMS,
            cost_estimate=CHEAP,
        )(place, after(w_gate, outgoing), w_up)
        wd = [cuts[0]]
        for (by, other), v in zip(MOVES[1:], cuts[1:]):
            pairs = [
                (i * n_core + c, (i + by) % n_y * n_core + (1 - c if other else c))
                for i in range(n_y)
                for c in range(n_core)
            ]
            if len(wd) == 7:
                v = after(v, other_g)
            wd.append(lax.ppermute(v, ("y", "core"), pairs))

    def exchange(v):
        return lax.all_to_all(v.reshape(n_dp, ROWS, v.shape[-1]), DP, 0, 0, tiled=True).reshape(v.shape)

    with jax.named_scope("dispatch"):
        arrived = exchange(outgoing)

    with jax.named_scope("scales"):
        both = jnp.stack([gate_scale, up_scale])
        own = lax.dynamic_index_in_dim(both, core, 1, keepdims=False)
        other = lax.ppermute(lax.dynamic_index_in_dim(both, 1 - core, 1, keepdims=False), "core", swap)
        scales = jnp.concatenate([own, other], axis=1)

    with jax.named_scope("unpack"):
        x_p, x_q, kv_q = pl.pallas_call(
            unpack_kernel,
            out_shape=[sds(rows, quarter), sds(rows + rows // 2, quarter), sds(rows, kv_cols)],
            compiler_params=PARAMS,
            cost_estimate=CHEAP,
        )(after(arrived, *wd[:6], scales), page_slots.reshape(1, -1))

    def shift(v, by):
        return lax.ppermute(v, "y", [(i, (i + by) % n_y) for i in range(n_y)])

    with jax.named_scope("rows"):
        x_p = after(x_p, x_q, *wd[6:])
        p_left, p_right = shift(x_p, 1), shift(x_p, -1)
        p_far = shift(p_left, 1)
        q_right = shift(after(x_q, p_right, p_left), -1)
        q_left = shift(after(x_q, p_far), 1)
        q_far = shift(q_right, -1)

    with jax.named_scope("swap"):
        w2 = [lax.ppermute(w, "core", swap) for w in (other_g, other_u)]

    units = n_core * hid

    def columns(k, p, steps):
        by = steps[0]
        for i, s in enumerate(steps[1:], 1):
            by = jnp.where(k == i, s, by)
        return lax.rem(p[0] + by, n_y)

    def weight_specs(*steps):
        def own():
            return pl.BlockSpec((1, hid, quarter), lambda k, p: (p[1], 0, columns(k, p, steps)))

        def other():
            return pl.BlockSpec((1, hid, quarter), lambda k, p: (0, 0, columns(k, p, steps)))

        return [own(), other(), own(), other()]

    def call(kernel, steps, in_specs, out_specs, out_shape, scratch=(), params=PARAMS):
        return pl.pallas_call(
            kernel,
            grid_spec=pltpu.PrefetchScalarGridSpec(
                num_scalar_prefetch=1,
                grid=(steps,),
                in_specs=in_specs,
                out_specs=out_specs,
                scratch_shapes=list(scratch),
            ),
            out_shape=out_shape,
            compiler_params=params,
            cost_estimate=CHEAP,
        )

    weights = (w_gate, w2[0], w_up, w2[1])
    channel = pl.BlockSpec((1, 1, quarter), lambda k, p: (p[1], 0, p[0]))
    down_scale = down_scale.reshape(experts, 1, width)

    def acc(r):
        return [pltpu.VMEM((r, 2 * units), F32)]

    with jax.named_scope("up"):
        r = rows
        both_p = call(
            up_first_kernel,
            3,
            [whole(r, quarter)] * 3 + weight_specs(0, 3, 1),
            whole(r, 2 * units),
            sds(r, 2 * units, dtype=F32),
        )(place, x_p, p_left, p_right, *weights)
        h_p = call(
            up_last_kernel,
            1,
            [whole(r, quarter)] + weight_specs(2) + [whole(r, 2 * units), whole(2, units)],
            whole(r, units),
            sds(r, units),
            acc(r),
        )(place, p_far, *weights, both_p, scales)

    with jax.named_scope("up"):
        r = rows + rows // 2
        both_q = call(
            up_first_kernel,
            2,
            [whole(r, quarter)] * 2 + weight_specs(0, 1),
            whole(r, 2 * units),
            sds(r, 2 * units, dtype=F32),
        )(place, x_q, q_right, *weights)
    with jax.named_scope("down"):
        near = [shift(h_p, 1), shift(h_p, -1), shift(h_p, 2)]
        near[2] = after(near[2], both_q)
        r = rows
        v_p = call(
            down_kernel,
            1,
            [whole(r, units)] * 4 + [whole(hid, quarter)] * 8 + [channel],
            whole(r, quarter),
            sds(r, quarter),
        )(place, h_p, *near, *wd, down_scale)
        back_p = exchange(v_p)

    with jax.named_scope("up"):
        r = rows + rows // 2
        h_q = call(
            up_last_kernel,
            2,
            [whole(r, quarter)] * 2 + weight_specs(3, 2) + [whole(r, 2 * units), whole(2, units)],
            whole(r, units),
            sds(r, units),
            acc(r),
        )(place, q_left, q_far, *weights, both_q, scales)

    with jax.named_scope("down"):
        near = [shift(h_q, 1), shift(h_q, -1), shift(h_q, 2)]
        part = pl.pallas_call(
            down_first_kernel,
            out_shape=sds(r, quarter, dtype=F32),
            compiler_params=SMALL,
            cost_estimate=CHEAP,
        )(h_q, *wd[:2])
        v_q = call(
            down_last_kernel,
            1,
            [whole(r, units)] * 3
            + [whole(hid, quarter)] * 6
            + [whole(r, quarter), channel, whole(rows, kv_cols)],
            whole(rows, payload),
            sds(rows, payload),
            params=SMALL,
        )(place, *near, *wd[2:], part, down_scale, kv_q)
        back_q = exchange(v_q)

    with jax.named_scope("combine"):
        total, picked = pl.pallas_call(
            functools.partial(combine_first_kernel, n_dp),
            in_specs=[smem] + [vmem] * 3,
            out_shape=[sds(tok, quarter, dtype=F32), sds(6, rows, tok)],
            compiler_params=SMALL,
            cost_estimate=CHEAP,
        )(place, ids_t, gates_t, back_p)
        keep, send, kv_cache = pl.pallas_call(
            combine_last_kernel,
            in_specs=[smem] + [vmem] * 3,
            out_shape=[sds(tok, half, dtype=F32), sds(tok, half, dtype=F32), sds(tok, kv_cols)],
            compiler_params=SMALL,
            cost_estimate=CHEAP,
        )(place, picked, total, back_q)
        moe_out = (keep + lax.ppermute(send, "core", [(0, 1), (1, 0)])).astype(BF)
    return moe_out, kv_cache.reshape(tok // PAGE, PAGE, kv_cols)


def solution(mesh):
    shape = mesh.devices.shape
    n_z, n_x, n_y = 8, 4, 4
    fine = Mesh(np.asarray(mesh.devices).reshape(n_z, n_x, n_y, shape[1] // n_y), ("z", "x", "y", "core"))
    group = ("y", "core")
    placed = (
        P(DP, None),
        P(DP, None),
        P(DP, None),
        P(DP, group, None),
        P(DP, group, None),
        P(DP, group, None),
        P(DP, group),
        P(DP, group),
        P(DP, None),
        P(DP, group),
        P(),
    )
    return jax.shard_map(
        on_device,
        mesh=fine,
        in_specs=placed,
        out_specs=(P(DP, group), P(DP, None, group)),
        check_vma=False,
    )
```
